128 devices in a mesh: px: 8 (over y_hi, x), py: 16 (over z, y_lo, core).
Axes of the slice: x: 4, y: 4 (y_hi: 2, y_lo: 2; y = y_hi * 2 + y_lo), z: 4, core: 2. Of those that a mesh axis runs over, the one named last changes fastest.
Arguments:
- out_grad: float32 [4, 32, 128, 128, 128], P(None, None, 'px', 'py'), may hold values from -6 to 6
- input_modes: bfloat16 [4, 32, 64, 64, 66], P(None, None, 'px', 'py'), may hold values from -6 to 6
- mode_weights: bfloat16 [32, 32, 64, 64, 66], P(None, None, 'px', 'py'), may hold values from -1 to 1
Outputs:
- weight_grad: bfloat16 [32, 32, 64, 64, 66], P(None, None, 'px', 'py')
- input_grad: bfloat16 [4, 32, 128, 128, 128], P(None, None, 'px', 'py')
The draws below stay inside these ranges and needn't reach their ends.
All inputs are finite; a program needn't handle non-finite values.
Results may differ from the reference program's by a relative error of at most 0.0057.
Values may be sent and summed in bfloat16 or wider, within the bound.
A program may use at most 192 MiB of HBM per device.

```python
import math
import jax
import jax.numpy as jnp
from jax import lax

BATCH = 4
CHAN = 32
NX = 128
NY = 128
NZ = 128
KXM = 64
KYM = 64
KZM = 33


def steps_of(key, extent, split, smallest, largest):
    gain = 1.0
    for dim, parts in split:
        heights = jax.random.uniform(jax.random.fold_in(jax.random.fold_in(key, 6), dim), (parts,), jnp.float32, smallest / len(split), largest / len(split))
        gain = gain * jnp.repeat(jnp.exp(heights), extent[dim] // parts).reshape((-1,) + (1,) * (len(extent) - 1 - dim))
    return gain


def scatter_about(own_key, dims, spread, most, shards=(), held_as=jnp.bfloat16):
    result = jax.random.normal(own_key, dims, jnp.float32) * spread
    if len(shards) > 0:
        result = steps_of(own_key, dims, shards, -0.22, 0.18) * result
    return jnp.clip(result, min=-most, max=most).astype(held_as)


def setup_inputs(seed: int = 0) -> dict:
    key_list = jax.random.split(jax.random.key(seed), 4)
    out_grad = scatter_about(key_list[0], (BATCH, CHAN, NX, NY, NZ), 1.0, 6.0, ((2, 8), (3, 16)), jnp.float32)
    input_modes = scatter_about(key_list[1], (BATCH, CHAN, KXM, KYM, 2 * KZM), 1.0, 6.0, ((2, 8), (3, 16)))
    mode_weights = scatter_about(key_list[2], (CHAN, CHAN, KXM, KYM, 2 * KZM), CHAN ** -0.5, 1.0, ((2, 8), (3, 16)))
    return dict(out_grad=out_grad, input_modes=input_modes, mode_weights=mode_weights)


HIGH = lax.Precision.HIGHEST

def kept_wavenumbers(kept, length):
    counter = jnp.arange(kept, dtype=jnp.int32)
    return jnp.where(counter < kept // 2, counter, counter + (length - kept))

def twiddle_tables(wavenumbers, length):
    position = jnp.arange(length, dtype=jnp.int32)
    turn_count = wavenumbers[:, None] * position[None, :] % length
    phase_angle = turn_count.astype(jnp.float32) * jnp.float32(2.0 * math.pi / length)
    norm_factor = jnp.float32(1.0 / math.sqrt(length))
    return (jnp.cos(phase_angle) * norm_factor, jnp.sin(phase_angle) * norm_factor)

def z_tables(kept, length):
    cosine, sine = twiddle_tables(jnp.arange(kept, dtype=jnp.int32), length)
    forward_z = jnp.concatenate([cosine.T, -sine.T], axis=1)
    weighting = jnp.where(jnp.arange(kept) == 0, 1.0, 2.0).astype(jnp.float32)
    inverse_z = jnp.concatenate([weighting[:, None] * cosine, -weighting[:, None] * sine], axis=0)
    return (forward_z, inverse_z)

def complex_apply(data, cosine, sine, spec, sign):
    half = data.shape[-1] // 2
    real_part = data[..., :half]
    imag_part = data[..., half:]
    out_real = jnp.einsum(spec, real_part, cosine, precision=HIGH) - sign * jnp.einsum(spec, imag_part, sine, precision=HIGH)
    out_imag = jnp.einsum(spec, imag_part, cosine, precision=HIGH) + sign * jnp.einsum(spec, real_part, sine, precision=HIGH)
    return jnp.concatenate([out_real, out_imag], axis=-1)

def reference(out_grad, input_modes, mode_weights):
    forward_z, inverse_z = z_tables(KZM, NZ)
    cos_x, sin_x = twiddle_tables(kept_wavenumbers(KXM, NX), NX)
    cos_y, sin_y = twiddle_tables(kept_wavenumbers(KYM, NY), NY)

    def forward_one(sample):
        grad_z = jnp.einsum('cxyz,zk->cxyk', sample, forward_z, precision=HIGH)
        grad_y = complex_apply(grad_z, cos_y, sin_y, 'cxyk,qy->cxqk', -1.0)
        return complex_apply(grad_y, cos_x, sin_x, 'cxqk,px->cpqk', -1.0).astype(jnp.bfloat16)
    grad_modes = lax.map(forward_one, out_grad)
    half = KZM
    grads = grad_modes.astype(jnp.float32)
    inputs = input_modes.astype(jnp.float32)
    weights = mode_weights.astype(jnp.float32)
    g_real, g_imag = (grads[..., :half], grads[..., half:])
    x_real, x_imag = (inputs[..., :half], inputs[..., half:])
    w_real, w_imag = (weights[..., :half], weights[..., half:])
    spec_w = 'bixyk,boxyk->ioxyk'
    dw_real = jnp.einsum(spec_w, x_real, g_real, precision=HIGH) + jnp.einsum(spec_w, x_imag, g_imag, precision=HIGH)
    dw_imag = jnp.einsum(spec_w, x_real, g_imag, precision=HIGH) - jnp.einsum(spec_w, x_imag, g_real, precision=HIGH)
    weight_grad = jnp.concatenate([dw_real, dw_imag], axis=-1).astype(jnp.bfloat16)
    spec_d = 'ioxyk,boxyk->bixyk'
    dm_real = jnp.einsum(spec_d, w_real, g_real, precision=HIGH) + jnp.einsum(spec_d, w_imag, g_imag, precision=HIGH)
    dm_imag = jnp.einsum(spec_d, w_real, g_imag, precision=HIGH) - jnp.einsum(spec_d, w_imag, g_real, precision=HIGH)
    mode_grad = jnp.concatenate([dm_real, dm_imag], axis=-1).astype(jnp.bfloat16)

    def inverse_one(sample):
        back_x = complex_apply(sample.astype(jnp.float32), cos_x, sin_x, 'cpqk,px->cxqk', 1.0)
        back_y = complex_apply(back_x, cos_y, sin_y, 'cxqk,qy->cxyk', 1.0)
        return jnp.einsum('cxyk,kz->cxyz', back_y, inverse_z, precision=HIGH).astype(jnp.bfloat16)
    input_grad = lax.map(inverse_one, mode_grad)
    return (weight_grad, input_grad)
```

```python
import math

import jax
import jax.numpy as jnp
import ml_dtypes
import numpy as np
from jax import lax
from jax.experimental import pallas as pl
from jax.experimental.pallas import tpu as pltpu
from jax.sharding import PartitionSpec as P

BF = jnp.bfloat16
F32 = jnp.float32
MESH = pl.DeviceIdType.MESH
N = 128
KEPT = 64
KZ = 33
PX = 8
PY = 16
MR = 144
CR = 272
T1, T2, G, GS = 0, 16, 32, 48


def split(table):
    high = table.astype(ml_dtypes.bfloat16)
    low = (table - high.astype(np.float64)).astype(ml_dtypes.bfloat16)
    return high, low


def tables():
    bf = ml_dtypes.bfloat16
    grid = np.arange(N)
    angle_z = 2 * math.pi * (np.outer(np.arange(KZ), grid) % N) / N
    norm = 1.0 / math.sqrt(N)
    cz, sz = np.cos(angle_z) * norm, np.sin(angle_z) * norm
    kept = np.concatenate([np.arange(KEPT // 2), np.arange(N - KEPT // 2, N)])
    angle = 2 * math.pi * (np.outer(kept, grid) % N) / N
    cos, sin = np.cos(angle) * norm, np.sin(angle) * norm

    fz = np.stack([cz, -sz], axis=1).reshape(2 * KZ, N)
    hi, lo = split(fz)
    zf = np.zeros((144, 256), bf)
    zf[:66, :128] = hi
    zf[:66, 128:] = hi
    zf[72:138, :128] = lo
    weight = np.where(np.arange(KZ) == 0, 1.0, 2.0)[:, None]
    iz = np.stack([weight * cz, -weight * sz], axis=1).reshape(2 * KZ, N)
    hi, lo = split(iz)
    zi = np.zeros((2, 72, N), bf)
    zi[0, :66] = hi
    zi[1, :66] = lo

    full = np.zeros((2, KEPT, 2, N))
    full[0, :, 0] = cos
    full[0, :, 1] = sin
    full[1, :, 0] = -sin
    full[1, :, 1] = cos

    wy = full.reshape(2, PX, 8, 2, PY, 8).transpose(1, 0, 2, 4, 3, 5).reshape(128, 256)
    hi, lo = split(wy)
    yf = np.concatenate([hi, lo], axis=0)
    yi = np.concatenate([hi.T, lo.T], axis=1)

    wx = full.reshape(2, PX, 8, 2, PX, 16).transpose(3, 4, 5, 1, 0, 2)
    hi, lo = split(wx)
    xf = np.zeros((2, 2, PX, 8, 16, PX, 2, 8, 8), bf)
    for bc in range(8):
        xf[0, :, :, bc, :, :, :, bc, :] = hi
        xf[1, :, :, bc, :, :, :, bc, :] = lo
    xf = xf.reshape(2, 2048, 1024)

    perm = np.zeros((2, MR, CR), bf)
    for h in range(2):
        for k in range(KZ):
            for r in range(4):
                perm[h, 4 * k + r, 8 * k + 4 * h + r] = 1
    perm = perm.reshape(2 * MR, CR)
    permt = np.ascontiguousarray(perm.T)

    place = np.zeros((2, MR, 4, 2, 128), bf)
    back = np.zeros((MR, 4, 128), bf)
    for k in range(KZ):
        for r in range(4):
            place[0, 4 * k + r, r, 0, k] = 1
            place[1, 4 * k + r, r, 0, KZ + k] = 1
            place[1, 4 * k + r, r, 1, k] = 1
            place[0, 4 * k + r, r, 1, KZ + k] = -1
            back[4 * k + r, r, k] = 1
    place = place.reshape(2, MR, 1024)
    back = back.reshape(MR, 512)

    dup = np.zeros((2 * KZ, 2, 128), bf)
    for k in range(KZ):
        for part in range(2):
            dup[part * KZ + k, part, k] = 1
            dup[part * KZ + k, part, KZ + k] = 1
    dup = dup.reshape(2 * KZ, 256)
    return zf, zi, yf, yi, xf, perm, permt, place, back, dup


def dot(a, b):
    return jnp.dot(a, b, preferred_element_type=F32)


def dot_nt(a, b):
    return lax.dot_general(a, b, (((1,), (1,)), ((), ())), preferred_element_type=F32)


def kernel(
    og, xm, w_hbm, xf_hbm, zf, zi, yf, yi, perm, permt, place, back, dup,
    wg, ig,
    ogv, wv, xfv, send_a, recv_a, send_b, recv_b, send_m, recv_m, send_n, recv_n,
    lines, dm, xr, xi, blk, turn, outv,
    og_sem, w_sem, xf_sem, wg_sem, ig_sem, self_sem,
    sa_sem, ra_sem, sb_sem, rb_sem, sm_sem, rm_sem,
    sn_sem, rn_sem, sc_sem, rc_sem, sd_sem, rd_sem,
):
    px = lax.axis_index("px")
    py = lax.axis_index("py")
    owner_px = py // 2

    for k in range(PY):
        chunk = lax.rem(py + 1 + k, PY)
        pltpu.make_async_copy(og.at[:, chunk], ogv.at[pl.ds(chunk * 4, 4)], og_sem.at[chunk]).start()
    pltpu.make_async_copy(xf_hbm, xfv, xf_sem).start()
    pltpu.make_async_copy(w_hbm, wv, w_sem).start()

    barrier = pltpu.get_barrier_semaphore()
    mine = jnp.where(owner_px == px, 1, 0)

    def greet_py(s, c):
        pl.semaphore_signal(barrier, inc=1, device_id=(px, lax.rem(py + s, PY)), device_id_type=MESH)
        return c

    def greet_px(s, c):
        pl.semaphore_signal(barrier, inc=1, device_id=(lax.rem(px + s, PX), py), device_id_type=MESH)
        return c

    def greet_m(t, c):
        to_x, to_y = t // 2, 2 * px + lax.rem(t, 2)

        @pl.when(jnp.logical_not(jnp.logical_and(to_x == px, to_y == py)))
        def _():
            pl.semaphore_signal(barrier, inc=1, device_id=(to_x, to_y), device_id_type=MESH)

        @pl.when(jnp.logical_not(jnp.logical_and(owner_px == px, t == py)))
        def _():
            pl.semaphore_signal(barrier, inc=1, device_id=(owner_px, t), device_id_type=MESH)

        return c

    lax.fori_loop(1, PY, greet_py, 0)
    lax.fori_loop(1, PX, greet_px, 0)
    lax.fori_loop(0, PY, greet_m, 0)

    def copy_a(s):
        to = lax.rem(py + s, PY)
        return pltpu.make_async_remote_copy(
            src_ref=send_a.at[to], dst_ref=recv_a.at[py], send_sem=sa_sem.at[to], recv_sem=ra_sem.at[py],
            device_id=(px, to), device_id_type=MESH)

    def arrive_a(src):
        return pltpu.make_async_remote_copy(
            src_ref=send_a.at[src], dst_ref=recv_a.at[src], send_sem=sa_sem.at[src], recv_sem=ra_sem.at[src],
            device_id=(px, src), device_id_type=MESH)

    def copy_b(s):
        to = lax.rem(px + s, PX)
        return pltpu.make_async_remote_copy(
            src_ref=send_b.at[to], dst_ref=recv_b.at[px], send_sem=sb_sem.at[to], recv_sem=rb_sem.at[px],
            device_id=(to, py), device_id_type=MESH)

    def arrive_b(src):
        return pltpu.make_async_remote_copy(
            src_ref=send_b.at[src], dst_ref=recv_b.at[src], send_sem=sb_sem.at[src], recv_sem=rb_sem.at[src],
            device_id=(src, py), device_id_type=MESH)

    def copy_m(to_x, h):
        return pltpu.make_async_remote_copy(
            src_ref=send_m.at[to_x, h], dst_ref=recv_m.at[py], send_sem=sm_sem.at[to_x, h], recv_sem=rm_sem.at[py],
            device_id=(to_x, 2 * px + h), device_id_type=MESH)

    def copy_n(to_y):
        h = lax.rem(py, 2)
        return pltpu.make_async_remote_copy(
            src_ref=send_n.at[to_y], dst_ref=recv_n.at[px, h], send_sem=sn_sem.at[to_y], recv_sem=rn_sem.at[px, h],
            device_id=(owner_px, to_y), device_id_type=MESH)

    def copy_c(s):
        to = lax.rem(px + s, PX)
        return pltpu.make_async_remote_copy(
            src_ref=send_b.at[PX + to], dst_ref=recv_b.at[PX + px], send_sem=sc_sem.at[to], recv_sem=rc_sem.at[px],
            device_id=(to, py), device_id_type=MESH)

    def arrive_c(src):
        return pltpu.make_async_remote_copy(
            src_ref=send_b.at[PX + src], dst_ref=recv_b.at[PX + src], send_sem=sc_sem.at[src], recv_sem=rc_sem.at[src],
            device_id=(src, py), device_id_type=MESH)

    def copy_d(s):
        to = lax.rem(py + s, PY)
        return pltpu.make_async_remote_copy(
            src_ref=send_a.at[PY + to], dst_ref=recv_a.at[PY + py], send_sem=sd_sem.at[to], recv_sem=rd_sem.at[py],
            device_id=(px, to), device_id_type=MESH)

    def arrive_d(src):
        return pltpu.make_async_remote_copy(
            src_ref=send_a.at[PY + src], dst_ref=recv_a.at[PY + src], send_sem=sd_sem.at[src], recv_sem=rd_sem.at[src],
            device_id=(px, src), device_id_type=MESH)

    def z_forward(chunk):
        pltpu.make_async_copy(og.at[:, chunk], ogv.at[pl.ds(chunk * 4, 4)], og_sem.at[chunk]).wait()
        for jj in range(4):
            parts = []
            for j in (2 * jj, 2 * jj + 1):
                for b in range(4):
                    parts.append(ogv[chunk * 4 + b, pl.ds(j, 32, stride=8), :])
            rows = jnp.concatenate(parts, axis=0)
            high = rows.astype(BF)
            low = (rows - high.astype(F32)).astype(BF)
            both = dot_nt(zf[...], jnp.concatenate([high, low], axis=1))
            res = both[0:72] + both[72:144]
            blk[pl.ds(2 * jj, 72, stride=8), :] = res[:, 0:128]
            blk[pl.ds(2 * jj + 1, 72, stride=8), :] = res[:, 128:256]

    def step_a(s, c):
        to = lax.rem(py + s, PY)
        z_forward(to)
        send_a[to] = blk[0:528, :].reshape(KZ, 16, 128).astype(BF)

        @pl.when(s == 1)
        def _():
            pl.semaphore_wait(barrier, 15 + 7 + 32 - 2 * mine)

        copy_a(s).start()
        return c

    lax.fori_loop(1, PY, step_a, 0)
    z_forward(py)
    recv_a[py] = blk[0:528, :].reshape(KZ, 16, 128).astype(BF)

    def widen(k, c):
        rows = pl.ds(pl.multiple_of(k * 256, 256), 256)
        both = dot(xm[rows, :], dup[...])
        xr[rows, :] = both[:, 0:128]
        xi[rows, :] = both[:, 128:256]
        ogv[T1 + k] = jnp.zeros((256, 128), F32)
        ogv[T2 + k] = jnp.zeros((256, 128), F32)
        return c

    lax.fori_loop(0, 16, widen, 0)

    def wait_a(s, c):
        arrive_a(lax.rem(py + PY - s, PY)).wait_recv()
        return c

    lax.fori_loop(1, PY, wait_a, 0)

    def step_b(k, c):
        data = recv_a[0:PY, k].reshape(256, 128)
        both = dot(yf[...], data)
        res = (both[0:128] + both[128:256]).astype(BF)
        send_b[0:PX, k] = res.reshape(PX, 16, 128)
        return c

    lax.fori_loop(0, KZ, step_b, 0, unroll=3)

    def start_b(s, c):
        copy_b(s).start()
        return c

    lax.fori_loop(1, PX, start_b, 0)
    pltpu.make_async_copy(xf_hbm, xfv, xf_sem).wait()

    def gather_b(src, data):
        data = data.astype(F32).reshape(KZ, 2, 8, 128)
        for ri in range(2):
            part = jnp.concatenate([data[:, ri].reshape(264, 128), jnp.zeros((8, 128), F32)], axis=0)
            lines[:, pl.ds(pl.multiple_of((ri * PX + src) * 128, 128), 128)] = part.astype(BF)

    def step_gather(s, c):
        src = lax.rem(px + PX - s, PX)
        arrive_b(src).wait_recv()
        gather_b(src, recv_b[src])
        return c

    gather_b(px, send_b[px])
    lax.fori_loop(1, PX, step_gather, 0)

    def step_c(k, c):
        cols = pl.ds(pl.multiple_of(k * 256, 256), 256)
        res = dot(lines[...], xfv[0, :, cols]) + dot(lines[...], xfv[1, :, cols])
        moved = dot(perm[...], res.astype(BF)).astype(BF)
        for e in range(2):
            send_m[2 * k + e] = moved[:, e * 128:(e + 1) * 128].reshape(2, MR, 128)
        for e in range(2):
            for h in range(2):
                own = jnp.logical_and(2 * k + e == px, 2 * px + h == py)

                @pl.when(jnp.logical_not(own))
                def _():
                    copy_m(2 * k + e, h).start()

                @pl.when(own)
                def _():
                    local = pltpu.make_async_copy(send_m.at[2 * k + e, h], recv_m.at[py], self_sem)
                    local.start()
                    local.wait()
        return c

    lax.fori_loop(0, 4, step_c, 0)

    def step_place(src, c):
        @pl.when(jnp.logical_not(jnp.logical_and(owner_px == px, src == py)))
        def _():
            pltpu.make_async_remote_copy(
                src_ref=send_m.at[0, 0], dst_ref=recv_m.at[src], send_sem=sm_sem.at[0, 0], recv_sem=rm_sem.at[src],
                device_id=(owner_px, src), device_id_type=MESH).wait_recv()

        turned = recv_m[src].astype(F32).T.astype(BF)
        res = dot(turned[0:64], place[0]) + dot(turned[64:128], place[1])
        for r in range(4):
            rows = pl.ds(r, 64, stride=4)
            ogv[G + src, rows, :] = res[:, r * 256:r * 256 + 128]
            ogv[GS + src, rows, :] = res[:, r * 256 + 128:r * 256 + 256]
        return c

    lax.fori_loop(0, PY, step_place, 0)
    pltpu.make_async_copy(w_hbm, wv, w_sem).wait()

    def step_modes(k, c):
        pair, half = k // 2, lax.rem(k, 2)
        off = pl.multiple_of(half * 16, 16)

        def add(op, acc):
            acc = list(acc)
            for oo in range(2):
                w = [wv[2 * pair + ii, 2 * op + oo, pl.ds(off, 16), :].astype(F32) for ii in range(2)]
                for b in range(4):
                    rows = pl.ds(pl.multiple_of((b * 2 + oo) * 32 + off, 16), 16)
                    gb = ogv[G + op, rows, 0:66]
                    sb = ogv[GS + op, rows, 0:66]
                    for ii in range(2):
                        n = (ii * 4 + b) * 2
                        acc[n] = acc[n] + w[ii] * gb
                        acc[n + 1] = acc[n + 1] + w[ii] * sb
            return tuple(acc)

        acc = lax.fori_loop(0, 16, add, tuple(jnp.zeros((16, 66), F32) for _ in range(16)))
        for ii in range(2):
            for b in range(4):
                rows = pl.ds(pl.multiple_of((b * 2 + ii) * 32 + off, 16), 16)
                ogv[T1 + pair, rows, 0:66] = acc[(ii * 4 + b) * 2]
                ogv[T2 + pair, rows, 0:66] = acc[(ii * 4 + b) * 2 + 1]
        return c

    def step_return(k, c):
        def rows_of(base, r):
            data = ogv[base + k, pl.ds(r, 64, stride=4), :]
            return data + pltpu.roll(data, 128 - KZ, 1)

        total = jnp.zeros((MR, 128), F32)
        for r in range(4):
            both = jnp.concatenate([rows_of(T1, r), rows_of(T2, r)], axis=0).astype(BF)
            total = total + dot_nt(back[:, r * 128:(r + 1) * 128], both)
        send_n[k] = total.astype(BF)
        own = jnp.logical_and(owner_px == px, k == py)

        @pl.when(jnp.logical_not(own))
        def _():
            copy_n(k).start()

        @pl.when(own)
        def _():
            local = pltpu.make_async_copy(send_n.at[k], recv_n.at[px, lax.rem(py, 2)], self_sem)
            local.start()
            local.wait()

        return c

    def step_pair(k, c):
        step_modes(2 * k, 0)
        step_modes(2 * k + 1, 0)
        return step_return(k, c)

    lax.fori_loop(0, 16, step_pair, 0)

    def step_weight(k, c):
        i, half = k // 2, lax.rem(k, 2)
        off = pl.multiple_of(half * 16, 16)
        xrb = [xr[pl.ds(pl.multiple_of((b * 32 + i) * 32 + off, 16), 16), 0:66] for b in range(4)]
        xib = [xi[pl.ds(pl.multiple_of((b * 32 + i) * 32 + off, 16), 16), 0:66] for b in range(4)]

        def one(op, c2):
            for oo in range(2):
                total = None
                for b in range(4):
                    rows = pl.ds(pl.multiple_of((b * 2 + oo) * 32 + off, 16), 16)
                    term = xrb[b] * ogv[G + op, rows, 0:66] + xib[b] * ogv[GS + op, rows, 0:66]
                    total = term if total is None else total + term
                wv[i, 2 * op + oo, pl.ds(off, 16), :] = total.astype(BF)
            return c2

        lax.fori_loop(0, 16, one, 0)

        @pl.when(half == 1)
        def _():
            pltpu.make_async_copy(wv.at[i], wg.at[i], wg_sem.at[i]).start()

        return c

    lax.fori_loop(0, 22, step_weight, 0)

    def step_unplace(k, c):
        for h in range(2):
            @pl.when(jnp.logical_not(jnp.logical_and(k == px, 2 * px + h == py)))
            def _():
                pltpu.make_async_remote_copy(
                    src_ref=send_n.at[0], dst_ref=recv_n.at[k, h], send_sem=sn_sem.at[0], recv_sem=rn_sem.at[k, h],
                    device_id=(k, 2 * px + h), device_id_type=MESH).wait_recv()

        moved = dot(permt[...], recv_n[k].reshape(2 * MR, 128))
        dm[:, pl.ds(pl.multiple_of(k * 128, 128), 128)] = moved.astype(BF)
        return c

    lax.fori_loop(0, PX, step_unplace, 0)

    def x_inverse(to):
        parts = []
        for ri in range(2):
            rows = pl.ds(pl.multiple_of((ri * PX + to) * 128, 128), 128)
            res = dot_nt(dm[...], xfv[0, rows, :]) + dot_nt(dm[...], xfv[1, rows, :])
            parts.append(res[0:264].reshape(KZ, 8, 128))
        return jnp.concatenate(parts, axis=1).astype(BF)

    def step_cb(s, c):
        to = lax.rem(px + s, PX)
        send_b[PX + to] = x_inverse(to)
        copy_c(s).start()
        return c

    lax.fori_loop(1, PX, step_cb, 0)
    recv_b[PX + px] = x_inverse(px)

    lax.fori_loop(22, 44, step_weight, 0)

    def wait_c(s, c):
        arrive_c(lax.rem(px + PX - s, PX)).wait_recv()
        return c

    lax.fori_loop(1, PX, wait_c, 0)

    def step_bb(k, c):
        data = recv_b[PX:2 * PX, k].reshape(128, 128)
        res = dot(yi[...], jnp.concatenate([data, data], axis=0)).astype(BF)
        send_a[PY:2 * PY, k] = res.reshape(PY, 16, 128)
        return c

    lax.fori_loop(0, KZ, step_bb, 0, unroll=3)

    def start_d(s, c):
        copy_d(s).start()
        return c

    lax.fori_loop(1, PY, start_d, 0)
    lax.fori_loop(44, 64, step_weight, 0)

    blk[528:576, :] = jnp.zeros((48, 128), F32)

    def z_inverse(src, data):
        blk[0:528, :] = data.astype(F32).reshape(528, 128)
        for j in range(8):
            turned = blk[pl.ds(j, 72, stride=8), :].T.astype(BF)
            res = dot(turned, zi[0]) + dot(turned, zi[1])
            turn[pl.ds(j, 128, stride=8), :] = res
        outv[src] = turn[...].reshape(4, 256, 128).astype(BF)
        pltpu.make_async_copy(outv.at[src], ig.at[:, src], ig_sem.at[src]).start()

    z_inverse(py, send_a[PY + py])

    def step_d(s, c):
        src = lax.rem(py + PY - s, PY)
        arrive_d(src).wait_recv()
        z_inverse(src, recv_a[PY + src])
        return c

    lax.fori_loop(1, PY, step_d, 0)

    def end_px(s, c):
        copy_b(s).wait_send()
        copy_c(s).wait_send()
        return c

    def end_py(s, c):
        copy_a(s).wait_send()
        copy_d(s).wait_send()
        return c

    def end_m(t, c):
        to_x, h = t // 2, lax.rem(t, 2)

        @pl.when(jnp.logical_not(jnp.logical_and(to_x == px, 2 * px + h == py)))
        def _():
            copy_m(to_x, h).wait_send()

        @pl.when(jnp.logical_not(jnp.logical_and(owner_px == px, t == py)))
        def _():
            copy_n(t).wait_send()

        pltpu.make_async_copy(outv.at[t], ig.at[:, t], ig_sem.at[t]).wait()
        return c

    def end_w(i, c):
        pltpu.make_async_copy(wv.at[i], wg.at[i], wg_sem.at[i]).wait()
        return c

    lax.fori_loop(1, PX, end_px, 0)
    lax.fori_loop(1, PY, end_py, 0)
    lax.fori_loop(0, PY, end_m, 0)
    lax.fori_loop(0, 32, end_w, 0)


def body(out_grad, input_modes, mode_weights):
    zf, zi, yf, yi, xf, perm, permt, place, back, dup = (jnp.asarray(t) for t in tables())
    og = out_grad.reshape(4, PY, 256, 128)
    xm = input_modes.reshape(4096, 66)
    w = mode_weights.reshape(32, 32, 32, 66)
    any_spec = pl.BlockSpec(memory_space=pl.ANY)
    vmem = pl.BlockSpec(memory_space=pltpu.VMEM)
    dma = pltpu.SemaphoreType.DMA
    wg, ig = pl.pallas_call(
        kernel,
        out_shape=(
            jax.ShapeDtypeStruct((32, 32, 32, 66), BF),
            jax.ShapeDtypeStruct((4, PY, 256, 128), BF),
        ),
        in_specs=[any_spec, vmem, any_spec, any_spec] + [vmem] * 9,
        out_specs=(any_spec, any_spec),
        scratch_shapes=[
            pltpu.VMEM((4 * PY, 256, 128), F32),
            pltpu.VMEM((32, 32, 32, 66), BF),
            pltpu.VMEM((2, 2048, 1024), BF),
            pltpu.VMEM((2 * PY, KZ, 16, 128), BF),
            pltpu.VMEM((2 * PY, KZ, 16, 128), BF),
            pltpu.VMEM((2 * PX, KZ, 16, 128), BF),
            pltpu.VMEM((2 * PX, KZ, 16, 128), BF),
            pltpu.VMEM((PX, 2, MR, 128), BF),
            pltpu.VMEM((PY, MR, 128), BF),
            pltpu.VMEM((PY, MR, 128), BF),
            pltpu.VMEM((PX, 2, MR, 128), BF),
            pltpu.VMEM((CR, 2048), BF),
            pltpu.VMEM((CR, 1024), BF),
            pltpu.VMEM((4096, 128), F32),
            pltpu.VMEM((4096, 128), F32),
            pltpu.VMEM((576, 128), F32),
            pltpu.VMEM((1024, 128), F32),
            pltpu.VMEM((PY, 4, 256, 128), BF),
            dma((PY,)), dma, dma, dma((32,)), dma((PY,)), dma,
            dma((PY,)), dma((PY,)), dma((PX,)), dma((PX,)), dma((PX, 2)), dma((PY,)),
            dma((PY,)), dma((PX, 2)), dma((PX,)), dma((PX,)), dma((PY,)), dma((PY,)),
        ],
        compiler_params=pltpu.CompilerParams(
            collective_id=0, has_side_effects=True, vmem_limit_bytes=54 * 1024 * 1024
        ),
    )(og, xm, w, xf, zf, zi, yf, yi, perm, permt, place, back, dup)
    return wg.reshape(32, 32, 8, 4, 66), ig.reshape(4, 32, 16, 8, 128)


def solution(mesh):
    spec = P(None, None, "px", "py", None)
    return jax.shard_map(
        body, mesh=mesh, in_specs=(spec, spec, spec), out_specs=(spec, spec), check_vma=False
    )
```

```python
import math

import jax
import jax.numpy as jnp
import ml_dtypes
import numpy as np
from jax import lax
from jax.experimental import pallas as pl
from jax.experimental.pallas import tpu as pltpu
from jax.sharding import PartitionSpec as P

BF = jnp.bfloat16
F32 = jnp.float32
MESH = pl.DeviceIdType.MESH
N = 128
KEPT = 64
KZ = 33
PX = 8
PY = 16
MR = 144
KG = 11
CR = 272
T1, T2, G, GS = 0, 16, 32, 48


def split(table):
    high = table.astype(ml_dtypes.bfloat16)
    low = (table - high.astype(np.float64)).astype(ml_dtypes.bfloat16)
    return high, low


def tables():
    bf = ml_dtypes.bfloat16
    grid = np.arange(N)
    angle_z = 2 * math.pi * (np.outer(np.arange(KZ), grid) % N) / N
    norm = 1.0 / math.sqrt(N)
    cz, sz = np.cos(angle_z) * norm, np.sin(angle_z) * norm
    kept = np.concatenate([np.arange(KEPT // 2), np.arange(N - KEPT // 2, N)])
    angle = 2 * math.pi * (np.outer(kept, grid) % N) / N
    cos, sin = np.cos(angle) * norm, np.sin(angle) * norm

    fz = np.stack([cz, -sz], axis=1).reshape(2 * KZ, N)
    hi, lo = split(fz)
    zf = np.zeros((144, 256), bf)
    zf[:66, :128] = hi
    zf[:66, 128:] = hi
    zf[72:138, :128] = lo
    weight = np.where(np.arange(KZ) == 0, 1.0, 2.0)[:, None]
    iz = np.stack([weight * cz, -weight * sz], axis=1).reshape(2 * KZ, N)
    hi, lo = split(iz)
    zi = np.zeros((2, 72, N), bf)
    zi[0, :66] = hi
    zi[1, :66] = lo

    full = np.zeros((2, KEPT, 2, N))
    full[0, :, 0] = cos
    full[0, :, 1] = sin
    full[1, :, 0] = -sin
    full[1, :, 1] = cos

    wy = full.reshape(2, PX, 8, 2, PY, 8).transpose(1, 0, 2, 4, 3, 5).reshape(128, 256)
    hi, lo = split(wy)
    yf = np.concatenate([hi, lo], axis=0)
    yi = np.concatenate([hi.T, lo.T], axis=1)

    wx = full.reshape(2, PX, 8, 2, PX, 16).transpose(3, 4, 5, 1, 0, 2)
    hi, lo = split(wx)
    xf = np.zeros((2, 2, PX, 8, 16, PX, 2, 8, 8), bf)
    for bc in range(8):
        xf[0, :, :, bc, :, :, :, bc, :] = hi
        xf[1, :, :, bc, :, :, :, bc, :] = lo
    xf = xf.reshape(2, 2048, 1024)

    perm = np.zeros((2, MR, CR), bf)
    for h in range(2):
        for k in range(KZ):
            for r in range(4):
                perm[h, 4 * k + r, 8 * k + 4 * h + r] = 1
    perm = perm.reshape(2 * MR, CR)
    permt = np.ascontiguousarray(perm.T)

    place = np.zeros((2, MR, 4, 2, 128), bf)
    back = np.zeros((MR, 4, 128), bf)
    for k in range(KZ):
        for r in range(4):
            place[0, 4 * k + r, r, 0, k] = 1
            place[1, 4 * k + r, r, 0, KZ + k] = 1
            place[1, 4 * k + r, r, 1, k] = 1
            place[0, 4 * k + r, r, 1, KZ + k] = -1
            back[4 * k + r, r, k] = 1
    place = place.reshape(2, MR, 1024)
    back = back.reshape(MR, 512)

    dup = np.zeros((2 * KZ, 2, 128), bf)
    for k in range(KZ):
        for part in range(2):
            dup[part * KZ + k, part, k] = 1
            dup[part * KZ + k, part, KZ + k] = 1
    dup = dup.reshape(2 * KZ, 256)
    return zf, zi, yf, yi, xf, perm, permt, place, back, dup


def dot(a, b):
    return jnp.dot(a, b, preferred_element_type=F32)


def dot_nt(a, b):
    return lax.dot_general(a, b, (((1,), (1,)), ((), ())), preferred_element_type=F32)


def kernel(
    og, xm, w_hbm, xf_hbm, zf, zi, yf, yi, perm, permt, place, back, dup,
    wg, ig,
    ogv, wv, xfv, send_a, recv_a, send_b, recv_b, send_m, recv_m, send_n, pass_n, recv_n,
    lines, dm, xr, xi, blk, turn, outv,
    og_sem, w_sem, xf_sem, wg_sem, ig_sem, self_sem,
    sa_sem, ra_sem, sb_sem, rb_sem, sm_sem, rm_sem,
    sn_sem, rn_sem, sp_sem, rp_sem, sc_sem, rc_sem, sd_sem, rd_sem,
):
    px = lax.axis_index("px")
    py = lax.axis_index("py")
    owner_px = py // 2

    for k in range(PY):
        chunk = lax.rem(py + 1 + k, PY)
        pltpu.make_async_copy(og.at[:, chunk], ogv.at[pl.ds(chunk * 4, 4)], og_sem.at[chunk]).start()
    pltpu.make_async_copy(xf_hbm, xfv, xf_sem).start()
    pltpu.make_async_copy(w_hbm, wv, w_sem).start()

    barrier = pltpu.get_barrier_semaphore()
    mine = jnp.where(owner_px == px, 1, 0)

    def greet_py(s, c):
        pl.semaphore_signal(barrier, inc=1, device_id=(px, lax.rem(py + s, PY)), device_id_type=MESH)
        return c

    def greet_px(s, c):
        pl.semaphore_signal(barrier, inc=1, device_id=(lax.rem(px + s, PX), py), device_id_type=MESH)
        return c

    def greet_m(t, c):
        to_x, to_y = t // 2, 2 * px + lax.rem(t, 2)

        @pl.when(jnp.logical_not(jnp.logical_and(to_x == px, to_y == py)))
        def _():
            pl.semaphore_signal(barrier, inc=1, device_id=(to_x, to_y), device_id_type=MESH)

        @pl.when(jnp.logical_not(jnp.logical_and(owner_px == px, t == py)))
        def _():
            pl.semaphore_signal(barrier, inc=1, device_id=(owner_px, t), device_id_type=MESH)

        return c

    lax.fori_loop(1, PY, greet_py, 0)
    lax.fori_loop(1, PX, greet_px, 0)
    lax.fori_loop(0, PY, greet_m, 0)

    def copy_a(s):
        to = lax.rem(py + s, PY)
        return pltpu.make_async_remote_copy(
            src_ref=send_a.at[to], dst_ref=recv_a.at[py], send_sem=sa_sem.at[to], recv_sem=ra_sem.at[py],
            device_id=(px, to), device_id_type=MESH)

    def arrive_a(src):
        return pltpu.make_async_remote_copy(
            src_ref=send_a.at[src], dst_ref=recv_a.at[src], send_sem=sa_sem.at[src], recv_sem=ra_sem.at[src],
            device_id=(px, src), device_id_type=MESH)

    def copy_b(s, part):
        to = lax.rem(px + s, PX)
        ks = pl.ds(part * KG, KG)
        return pltpu.make_async_remote_copy(
            src_ref=send_b.at[to, ks], dst_ref=recv_b.at[px, ks], send_sem=sb_sem.at[part, to],
            recv_sem=rb_sem.at[part, px], device_id=(to, py), device_id_type=MESH)

    def arrive_b(src, part):
        ks = pl.ds(part * KG, KG)
        return pltpu.make_async_remote_copy(
            src_ref=send_b.at[src, ks], dst_ref=recv_b.at[src, ks], send_sem=sb_sem.at[part, src],
            recv_sem=rb_sem.at[part, src], device_id=(src, py), device_id_type=MESH)

    def copy_m(to_x, h):
        return pltpu.make_async_remote_copy(
            src_ref=send_m.at[to_x, h], dst_ref=recv_m.at[py], send_sem=sm_sem.at[to_x, h], recv_sem=rm_sem.at[py],
            device_id=(to_x, 2 * px + h), device_id_type=MESH)

    def copy_n(to_y):
        return pltpu.make_async_remote_copy(
            src_ref=send_n.at[to_y], dst_ref=pass_n.at[py], send_sem=sn_sem.at[to_y], recv_sem=rn_sem.at[py],
            device_id=(px, to_y), device_id_type=MESH)

    def arrive_n(src):
        return pltpu.make_async_remote_copy(
            src_ref=send_n.at[src], dst_ref=pass_n.at[src], send_sem=sn_sem.at[src], recv_sem=rn_sem.at[src],
            device_id=(px, src), device_id_type=MESH)

    def copy_p(to):
        return pltpu.make_async_remote_copy(
            src_ref=pass_n.at[pl.ds(2 * to, 2)], dst_ref=recv_n.at[px], send_sem=sp_sem.at[to],
            recv_sem=rp_sem.at[px], device_id=(to, py), device_id_type=MESH)

    def arrive_p(src):
        return pltpu.make_async_remote_copy(
            src_ref=pass_n.at[pl.ds(2 * src, 2)], dst_ref=recv_n.at[src], send_sem=sp_sem.at[src],
            recv_sem=rp_sem.at[src], device_id=(src, py), device_id_type=MESH)

    def copy_c(s):
        to = lax.rem(px + s, PX)
        return pltpu.make_async_remote_copy(
            src_ref=send_b.at[PX + to], dst_ref=recv_b.at[PX + px], send_sem=sc_sem.at[to], recv_sem=rc_sem.at[px],
            device_id=(to, py), device_id_type=MESH)

    def arrive_c(src):
        return pltpu.make_async_remote_copy(
            src_ref=send_b.at[PX + src], dst_ref=recv_b.at[PX + src], send_sem=sc_sem.at[src], recv_sem=rc_sem.at[src],
            device_id=(src, py), device_id_type=MESH)

    def copy_d(s, part):
        to = lax.rem(py + s, PY)
        ks = pl.ds(part * KG, KG)
        return pltpu.make_async_remote_copy(
            src_ref=send_a.at[PY + to, ks], dst_ref=recv_a.at[PY + py, ks], send_sem=sd_sem.at[part, to],
            recv_sem=rd_sem.at[part, py], device_id=(px, to), device_id_type=MESH)

    def arrive_d(src, part):
        ks = pl.ds(part * KG, KG)
        return pltpu.make_async_remote_copy(
            src_ref=send_a.at[PY + src, ks], dst_ref=recv_a.at[PY + src, ks], send_sem=sd_sem.at[part, src],
            recv_sem=rd_sem.at[part, src], device_id=(px, src), device_id_type=MESH)

    def z_forward(chunk):
        pltpu.make_async_copy(og.at[:, chunk], ogv.at[pl.ds(chunk * 4, 4)], og_sem.at[chunk]).wait()
        for jj in range(4):
            parts = []
            for j in (2 * jj, 2 * jj + 1):
                for b in range(4):
                    parts.append(ogv[chunk * 4 + b, pl.ds(j, 32, stride=8), :])
            rows = jnp.concatenate(parts, axis=0)
            high = rows.astype(BF)
            low = (rows - high.astype(F32)).astype(BF)
            both = dot_nt(zf[...], jnp.concatenate([high, low], axis=1))
            res = both[0:72] + both[72:144]
            blk[pl.ds(2 * jj, 72, stride=8), :] = res[:, 0:128]
            blk[pl.ds(2 * jj + 1, 72, stride=8), :] = res[:, 128:256]

    def step_a(s, c):
        to = lax.rem(py + s, PY)
        z_forward(to)
        send_a[to] = blk[0:528, :].reshape(KZ, 16, 128).astype(BF)

        @pl.when(s == 1)
        def _():
            pl.semaphore_wait(barrier, 15 + 7 + 32 - 2 * mine)

        copy_a(s).start()
        return c

    lax.fori_loop(1, PY, step_a, 0)
    z_forward(py)
    recv_a[py] = blk[0:528, :].reshape(KZ, 16, 128).astype(BF)

    def widen(k, c):
        rows = pl.ds(pl.multiple_of(k * 256, 256), 256)
        both = dot(xm[rows, :], dup[...])
        xr[rows, :] = both[:, 0:128]
        xi[rows, :] = both[:, 128:256]
        ogv[T1 + k] = jnp.zeros((256, 128), F32)
        ogv[T2 + k] = jnp.zeros((256, 128), F32)
        return c

    lax.fori_loop(0, 16, widen, 0)

    def wait_a(s, c):
        arrive_a(lax.rem(py + PY - s, PY)).wait_recv()
        return c

    lax.fori_loop(1, PY, wait_a, 0)

    def step_b(k, c):
        data = recv_a[0:PY, k].reshape(256, 128)
        both = dot(yf[...], data)
        res = (both[0:128] + both[128:256]).astype(BF)
        send_b[0:PX, k] = res.reshape(PX, 16, 128)
        return c

    def part_b(part, c):
        lax.fori_loop(part * KG, part * KG + KG, step_b, 0, unroll=True)

        def start_b(s, c2):
            copy_b(s, part).start()
            return c2

        return lax.fori_loop(1, PX, start_b, c)

    lax.fori_loop(0, 3, part_b, 0)
    pltpu.make_async_copy(xf_hbm, xfv, xf_sem).wait()

    def gather_b(src, data):
        data = data.astype(F32).reshape(KZ, 2, 8, 128)
        for ri in range(2):
            part = jnp.concatenate([data[:, ri].reshape(264, 128), jnp.zeros((8, 128), F32)], axis=0)
            lines[:, pl.ds(pl.multiple_of((ri * PX + src) * 128, 128), 128)] = part.astype(BF)

    def step_gather(s, c):
        src = lax.rem(px + PX - s, PX)
        for part in range(3):
            arrive_b(src, part).wait_recv()
        gather_b(src, recv_b[src])
        return c

    gather_b(px, send_b[px])
    lax.fori_loop(1, PX, step_gather, 0)

    def step_c(k, c):
        pair = lax.rem(px // 2 + py + k, 4)
        cols = pl.ds(pl.multiple_of(pair * 256, 256), 256)
        res = dot(lines[...], xfv[0, :, cols]) + dot(lines[...], xfv[1, :, cols])
        moved = dot(perm[...], res.astype(BF)).astype(BF)
        for e in range(2):
            send_m[2 * pair + e] = moved[:, e * 128:(e + 1) * 128].reshape(2, MR, 128)
        for e in range(2):
            for h in range(2):
                own = jnp.logical_and(2 * pair + e == px, 2 * px + h == py)

                @pl.when(jnp.logical_not(own))
                def _():
                    copy_m(2 * pair + e, h).start()

                @pl.when(own)
                def _():
                    local = pltpu.make_async_copy(send_m.at[2 * pair + e, h], recv_m.at[py], self_sem)
                    local.start()
                    local.wait()
        return c

    lax.fori_loop(0, 4, step_c, 0)

    def senders(k):
        first = lax.rem(px // 2 + 8 - owner_px // 2 - k, 4)
        return [first + 4 * m for m in range(4)]

    def place_modes(k):
        real, imag = [], []
        for src in senders(k):
            @pl.when(jnp.logical_not(jnp.logical_and(owner_px == px, src == py)))
            def _():
                pltpu.make_async_remote_copy(
                    src_ref=send_m.at[0, 0], dst_ref=recv_m.at[src], send_sem=sm_sem.at[0, 0], recv_sem=rm_sem.at[src],
                    device_id=(owner_px, src), device_id_type=MESH).wait_recv()

            turned = recv_m[src].astype(F32).T.astype(BF)
            real.append(turned[0:64])
            imag.append(turned[64:128])
        real, imag = jnp.concatenate(real, axis=0), jnp.concatenate(imag, axis=0)
        for r in range(4):
            cols = slice(r * 256, r * 256 + 256)
            res = dot(real, place[0, :, cols]) + dot(imag, place[1, :, cols])
            for m, src in enumerate(senders(k)):
                rows = pl.ds(r, 64, stride=4)
                ogv[G + src, rows, :] = res[m * 64:m * 64 + 64, 0:128]
                ogv[GS + src, rows, :] = res[m * 64:m * 64 + 64, 128:256]

    pltpu.make_async_copy(w_hbm, wv, w_sem).wait()

    def step_modes(pair, off, k):
        tv, uv = ogv.at[T1 + pair], ogv.at[T2 + pair]
        acc = []
        for ii in range(2):
            for b in range(4):
                at = (b * 2 + ii) * 32 + off
                acc.append(tv[at:at + 16, 0:66])
                acc.append(uv[at:at + 16, 0:66])
        for src in senders(k):
            gv, sv = ogv.at[G + src], ogv.at[GS + src]
            wp = [wv.at[2 * pair + ii, pl.ds(2 * src, 2)] for ii in range(2)]
            for oo in range(2):
                w = [wp[ii][oo, off:off + 16, :].astype(F32) for ii in range(2)]
                for b in range(4):
                    at = (b * 2 + oo) * 32 + off
                    gb = gv[at:at + 16, 0:66]
                    sb = sv[at:at + 16, 0:66]
                    for ii in range(2):
                        n = (ii * 4 + b) * 2
                        acc[n] = acc[n] + w[ii] * gb
                        acc[n + 1] = acc[n + 1] + w[ii] * sb
        for ii in range(2):
            for b in range(4):
                at = (b * 2 + ii) * 32 + off
                tv[at:at + 16, 0:66] = acc[(ii * 4 + b) * 2]
                uv[at:at + 16, 0:66] = acc[(ii * 4 + b) * 2 + 1]

    def step_return(k, c):
        def rows_of(base, r):
            data = ogv[base + k, pl.ds(r, 64, stride=4), :]
            return data + pltpu.roll(data, 128 - KZ, 1)

        total = jnp.zeros((MR, 128), F32)
        for r in range(4):
            both = jnp.concatenate([rows_of(T1, r), rows_of(T2, r)], axis=0).astype(BF)
            total = total + dot_nt(back[:, r * 128:(r + 1) * 128], both)
        send_n[k] = total.astype(BF)

        @pl.when(k != py)
        def _():
            copy_n(k).start()

        @pl.when(k == py)
        def _():
            local = pltpu.make_async_copy(send_n.at[k], pass_n.at[py], self_sem)
            local.start()
            local.wait()

        return c

    def step_group(k, c):
        place_modes(k)

        def step_pair(pair, c2):
            step_modes(pair, 0, k)
            step_modes(pair, 16, k)
            return c2

        return lax.fori_loop(0, 16, step_pair, c)

    lax.fori_loop(0, 3, step_group, 0)
    place_modes(3)

    def step_last(s, c):
        pair = lax.rem(py + s, PY)
        step_modes(pair, 0, 3)
        step_modes(pair, 16, 3)
        return step_return(pair, c)

    lax.fori_loop(0, 16, step_last, 0)

    def step_weight(i, c):
        for off in (0, 16):
            xrb = [xr[pl.ds(pl.multiple_of((b * 32 + i) * 32 + off, 16), 16), 0:66] for b in range(4)]
            xib = [xi[pl.ds(pl.multiple_of((b * 32 + i) * 32 + off, 16), 16), 0:66] for b in range(4)]

            def one(op, c2):
                gv, sv, out = ogv.at[G + op], ogv.at[GS + op], wv.at[i, pl.ds(2 * op, 2)]
                for oo in range(2):
                    total = None
                    for b in range(4):
                        at = (b * 2 + oo) * 32 + off
                        term = xrb[b] * gv[at:at + 16, 0:66] + xib[b] * sv[at:at + 16, 0:66]
                        total = term if total is None else total + term
                    out[oo, off:off + 16, :] = total.astype(BF)
                return c2

            lax.fori_loop(0, 16, one, 0)

        pltpu.make_async_copy(wv.at[i], wg.at[i], wg_sem.at[i]).start()
        return c

    lax.fori_loop(0, 6, step_weight, 0)

    def step_pass(s, c):
        to = lax.rem(px + s, PX)
        for h in range(2):
            @pl.when(2 * to + h != py)
            def _():
                arrive_n(2 * to + h).wait_recv()

        @pl.when(s != PX)
        def _():
            copy_p(to).start()

        @pl.when(s == PX)
        def _():
            local = pltpu.make_async_copy(pass_n.at[pl.ds(2 * to, 2)], recv_n.at[px], self_sem)
            local.start()
            local.wait()

        return c

    lax.fori_loop(1, PX + 1, step_pass, 0)
    lax.fori_loop(6, 13, step_weight, 0)

    def step_unplace(s, c):
        src = lax.rem(px + PX - s, PX)

        @pl.when(s != 0)
        def _():
            arrive_p(src).wait_recv()

        moved = dot(permt[...], recv_n[src].reshape(2 * MR, 128))
        dm[:, pl.ds(pl.multiple_of(src * 128, 128), 128)] = moved.astype(BF)
        return c

    lax.fori_loop(0, PX, step_unplace, 0)

    def x_inverse(to):
        parts = []
        for ri in range(2):
            rows = pl.ds(pl.multiple_of((ri * PX + to) * 128, 128), 128)
            res = dot_nt(dm[...], xfv[0, rows, :]) + dot_nt(dm[...], xfv[1, rows, :])
            parts.append(res[0:264].reshape(KZ, 8, 128))
        return jnp.concatenate(parts, axis=1).astype(BF)

    def step_cb(s, c):
        to = lax.rem(px + s, PX)
        send_b[PX + to] = x_inverse(to)
        copy_c(s).start()
        return c

    lax.fori_loop(1, PX, step_cb, 0)
    recv_b[PX + px] = x_inverse(px)

    lax.fori_loop(13, 24, step_weight, 0)

    def wait_c(s, c):
        arrive_c(lax.rem(px + PX - s, PX)).wait_recv()
        return c

    lax.fori_loop(1, PX, wait_c, 0)

    def step_bb(k, c):
        data = recv_b[PX:2 * PX, k].reshape(128, 128)
        res = dot(yi[...], jnp.concatenate([data, data], axis=0)).astype(BF)
        send_a[PY:2 * PY, k] = res.reshape(PY, 16, 128)
        return c

    def part_d(part, c):
        lax.fori_loop(part * KG, part * KG + KG, step_bb, 0, unroll=True)

        def start_d(s, c2):
            copy_d(s, part).start()
            return c2

        return lax.fori_loop(1, PY, start_d, c)

    lax.fori_loop(0, 3, part_d, 0)
    lax.fori_loop(24, 32, step_weight, 0)

    blk[528:576, :] = jnp.zeros((48, 128), F32)

    def z_inverse(src, data):
        blk[0:528, :] = data.astype(F32).reshape(528, 128)
        for j in range(8):
            turned = blk[pl.ds(j, 72, stride=8), :].T.astype(BF)
            res = dot(turned, zi[0]) + dot(turned, zi[1])
            turn[pl.ds(j, 128, stride=8), :] = res
        outv[src] = turn[...].reshape(4, 256, 128).astype(BF)
        pltpu.make_async_copy(outv.at[src], ig.at[:, src], ig_sem.at[src]).start()

    z_inverse(py, send_a[PY + py])

    def step_d(s, c):
        src = lax.rem(py + PY - s, PY)
        for part in range(3):
            arrive_d(src, part).wait_recv()
        z_inverse(src, recv_a[PY + src])
        return c

    lax.fori_loop(1, PY, step_d, 0)

    def end_px(s, c):
        for part in range(3):
            copy_b(s, part).wait_send()
        copy_c(s).wait_send()
        copy_p(lax.rem(px + s, PX)).wait_send()
        return c

    def end_py(s, c):
        copy_a(s).wait_send()
        for part in range(3):
            copy_d(s, part).wait_send()
        copy_n(lax.rem(py + s, PY)).wait_send()
        return c

    def end_m(t, c):
        to_x, h = t // 2, lax.rem(t, 2)

        @pl.when(jnp.logical_not(jnp.logical_and(to_x == px, 2 * px + h == py)))
        def _():
            copy_m(to_x, h).wait_send()

        pltpu.make_async_copy(outv.at[t], ig.at[:, t], ig_sem.at[t]).wait()
        return c

    def end_w(i, c):
        pltpu.make_async_copy(wv.at[i], wg.at[i], wg_sem.at[i]).wait()
        return c

    lax.fori_loop(1, PX, end_px, 0)
    lax.fori_loop(1, PY, end_py, 0)
    lax.fori_loop(0, PY, end_m, 0)
    lax.fori_loop(0, 32, end_w, 0)


def hand_on(held, wg, buf, in_sem, out_sem):
    def load(i):
        return pltpu.make_async_copy(held.at[pl.ds(2 * i, 2)], buf.at[pl.ds(2 * i, 2)], in_sem.at[i])

    def store(i):
        return pltpu.make_async_copy(buf.at[pl.ds(2 * i, 2)], wg.at[pl.ds(2 * i, 2)], out_sem.at[i])

    for i in range(16):
        load(i).start()
    for i in range(16):
        load(i).wait()
        store(i).start()
    for i in range(16):
        store(i).wait()


def body(out_grad, input_modes, mode_weights):
    zf, zi, yf, yi, xf, perm, permt, place, back, dup = (jnp.asarray(t) for t in tables())
    og = out_grad.reshape(4, PY, 256, 128)
    xm = input_modes.reshape(4096, 66)
    w = mode_weights.reshape(32, 32, 32, 66)
    any_spec = pl.BlockSpec(memory_space=pl.ANY)
    vmem = pl.BlockSpec(memory_space=pltpu.VMEM)
    dma = pltpu.SemaphoreType.DMA
    wg, ig = pl.pallas_call(
        kernel,
        out_shape=(
            jax.ShapeDtypeStruct((32, 32, 32, 66), BF),
            jax.ShapeDtypeStruct((4, PY, 256, 128), BF),
        ),
        in_specs=[any_spec, vmem, any_spec, any_spec] + [vmem] * 9,
        out_specs=(any_spec, any_spec),
        scratch_shapes=[
            pltpu.VMEM((4 * PY, 256, 128), F32),
            pltpu.VMEM((32, 32, 32, 66), BF),
            pltpu.VMEM((2, 2048, 1024), BF),
            pltpu.VMEM((2 * PY, KZ, 16, 128), BF),
            pltpu.VMEM((2 * PY, KZ, 16, 128), BF),
            pltpu.VMEM((2 * PX, KZ, 16, 128), BF),
            pltpu.VMEM((2 * PX, KZ, 16, 128), BF),
            pltpu.VMEM((PX, 2, MR, 128), BF),
            pltpu.VMEM((PY, MR, 128), BF),
            pltpu.VMEM((PY, MR, 128), BF),
            pltpu.VMEM((PY, MR, 128), BF),
            pltpu.VMEM((PX, 2, MR, 128), BF),
            pltpu.VMEM((CR, 2048), BF),
            pltpu.VMEM((CR, 1024), BF),
            pltpu.VMEM((4096, 128), F32),
            pltpu.VMEM((4096, 128), F32),
            pltpu.VMEM((576, 128), F32),
            pltpu.VMEM((1024, 128), F32),
            pltpu.VMEM((PY, 4, 256, 128), BF),
            dma((PY,)), dma, dma, dma((32,)), dma((PY,)), dma,
            dma((PY,)), dma((PY,)), dma((3, PX)), dma((3, PX)), dma((PX, 2)), dma((PY,)),
            dma((PY,)), dma((PY,)), dma((PX,)), dma((PX,)), dma((PX,)), dma((PX,)), dma((3, PY)), dma((3, PY)),
        ],
        compiler_params=pltpu.CompilerParams(
            collective_id=0, has_side_effects=True, vmem_limit_bytes=54 * 1024 * 1024
        ),
    )(og, xm, w, xf, zf, zi, yf, yi, perm, permt, place, back, dup)
    wg = pl.pallas_call(
        hand_on,
        out_shape=jax.ShapeDtypeStruct((32, 32, 32, 66), BF),
        in_specs=[any_spec],
        out_specs=any_spec,
        scratch_shapes=[pltpu.VMEM((32, 32, 32, 66), BF), dma((16,)), dma((16,))],
        compiler_params=pltpu.CompilerParams(vmem_limit_bytes=54 * 1024 * 1024),
        cost_estimate=pl.CostEstimate(flops=0, bytes_accessed=17000000, transcendentals=0),
    )(wg)
    return wg.reshape(32, 32, 8, 4, 66), ig.reshape(4, 32, 16, 8, 128)


def solution(mesh):
    spec = P(None, None, "px", "py", None)
    return jax.shard_map(
        body, mesh=mesh, in_specs=(spec, spec, spec), out_specs=(spec, spec), check_vma=False
    )
```

```python
import math

import jax
import jax.numpy as jnp
import ml_dtypes
import numpy as np
from jax import lax
from jax.experimental import pallas as pl
from jax.experimental.pallas import tpu as pltpu
from jax.sharding import PartitionSpec as P

BF = jnp.bfloat16
F32 = jnp.float32
MESH = pl.DeviceIdType.MESH
N = 128
KEPT = 64
KZ = 33
PX = 8
PY = 16
MR = 144
W1, W2 = 7, 20
KG = 11
NR = 48
CR = 272
T1, T2, G, GS = 0, 16, 32, 48


def split(table):
    high = table.astype(ml_dtypes.bfloat16)
    low = (table - high.astype(np.float64)).astype(ml_dtypes.bfloat16)
    return high, low


def tables():
    bf = ml_dtypes.bfloat16
    grid = np.arange(N)
    angle_z = 2 * math.pi * (np.outer(np.arange(KZ), grid) % N) / N
    norm = 1.0 / math.sqrt(N)
    cz, sz = np.cos(angle_z) * norm, np.sin(angle_z) * norm
    kept = np.concatenate([np.arange(KEPT // 2), np.arange(N - KEPT // 2, N)])
    angle = 2 * math.pi * (np.outer(kept, grid) % N) / N
    cos, sin = np.cos(angle) * norm, np.sin(angle) * norm

    fz = np.stack([cz, -sz], axis=1).reshape(2 * KZ, N)
    hi, lo = split(fz)
    zf = np.zeros((144, 256), bf)
    zf[:66, :128] = hi
    zf[:66, 128:] = hi
    zf[72:138, :128] = lo
    weight = np.where(np.arange(KZ) == 0, 1.0, 2.0)[:, None]
    iz = np.stack([weight * cz, -weight * sz], axis=1).reshape(2 * KZ, N)
    hi, lo = split(iz)
    zi = np.zeros((2, 72, N), bf)
    zi[0, :66] = hi
    zi[1, :66] = lo

    full = np.zeros((2, KEPT, 2, N))
    full[0, :, 0] = cos
    full[0, :, 1] = sin
    full[1, :, 0] = -sin
    full[1, :, 1] = cos

    wy = full.reshape(2, PX, 8, 2, PY, 8).transpose(1, 0, 2, 4, 3, 5).reshape(128, 256)
    hi, lo = split(wy)
    yf = np.concatenate([hi, lo], axis=0)
    held = 4 * (2 * np.arange(8)[None, :] + np.arange(PX)[:, None] // 4) + np.arange(PX)[:, None] % 4
    wy = full[:, held.reshape(-1)].reshape(2, PX, 8, 2, PY, 8).transpose(1, 0, 2, 4, 3, 5).reshape(128, 256)
    hi, lo = split(wy)
    yi = np.concatenate([hi.T, lo.T], axis=1)

    wx = full.reshape(2, PX, 8, 2, PX, 16).transpose(4, 3, 5, 1, 0, 2)
    hi, lo = split(wx)
    xf = np.zeros((2, PX, 2, 8, 16, PX, 2, 8, 8), bf)
    for bc in range(8):
        xf[0, :, :, bc, :, :, :, bc, :] = hi
        xf[1, :, :, bc, :, :, :, bc, :] = lo
    xf = xf.reshape(2, 2048, 1024)

    perm = np.zeros((2, MR, CR), bf)
    for h in range(2):
        for k in range(KZ):
            for r in range(4):
                perm[h, 4 * k + r, 8 * k + 4 * h + r] = 1
    perm = perm.reshape(2 * MR, CR)
    permt = np.zeros((CR, 8, NR), bf)
    for t in range(8):
        for k in range(KZ):
            permt[8 * k + t, t, k] = 1
    permt = permt.reshape(CR, 8 * NR)

    place = np.zeros((2, MR, 4, 2, 128), bf)
    back = np.zeros((NR, 128), bf)
    for k in range(KZ):
        for r in range(4):
            place[0, 4 * k + r, r, 0, k] = 1
            place[1, 4 * k + r, r, 0, KZ + k] = 1
            place[1, 4 * k + r, r, 1, k] = 1
            place[0, 4 * k + r, r, 1, KZ + k] = -1
    place = place.reshape(2, MR, 1024)
    back[np.arange(KZ), np.arange(KZ)] = 1

    dup = np.zeros((2 * KZ, 2, 128), bf)
    for k in range(KZ):
        for part in range(2):
            dup[part * KZ + k, part, k] = 1
            dup[part * KZ + k, part, KZ + k] = 1
    dup = dup.reshape(2 * KZ, 256)
    return zf, zi, yf, yi, xf, perm, permt, place, back, dup


def dot(a, b):
    return jnp.dot(a, b, preferred_element_type=F32)


def dot_nt(a, b):
    return lax.dot_general(a, b, (((1,), (1,)), ((), ())), preferred_element_type=F32)


def kernel(
    og, xm, w_hbm, xf_hbm, zf, yf, yi, perm, permt, place, back, dup,
    wg, lines_out,
    ogv, wv, xfv, send_a, recv_a, send_b, recv_b, send_m, recv_m, send_n, recv_n,
    lines, sums, dm, xr, xi, blk,
    og_sem, w_sem, xf_sem, wg_sem, self_sem,
    sa_sem, ra_sem, sb_sem, rb_sem, sm_sem, rm_sem,
    sn_sem, rn_sem, sc_sem, rc_sem, sd_sem, rd_sem,
):
    px = lax.axis_index("px")
    py = lax.axis_index("py")
    owner_px = py // 2

    for k in range(PY):
        chunk = lax.rem(py + 1 + k, PY)
        pltpu.make_async_copy(og.at[:, chunk], ogv.at[pl.ds(chunk * 4, 4)], og_sem.at[chunk]).start()
    pltpu.make_async_copy(xf_hbm, xfv, xf_sem).start()
    pltpu.make_async_copy(w_hbm, wv, w_sem).start()

    barrier = pltpu.get_barrier_semaphore()
    me = px * PY + py

    def greet(k, c):
        to = lax.rem(me + k, PX * PY)
        pl.semaphore_signal(barrier, inc=1, device_id=(to // PY, lax.rem(to, PY)), device_id_type=MESH)
        return c

    lax.fori_loop(1, PX * PY, greet, 0)

    def copy_a(s):
        to = lax.rem(py + s, PY)
        return pltpu.make_async_remote_copy(
            src_ref=send_a.at[to], dst_ref=recv_a.at[py], send_sem=sa_sem.at[to], recv_sem=ra_sem.at[py],
            device_id=(px, to), device_id_type=MESH)

    def arrive_a(src):
        return pltpu.make_async_remote_copy(
            src_ref=send_a.at[src], dst_ref=recv_a.at[src], send_sem=sa_sem.at[src], recv_sem=ra_sem.at[src],
            device_id=(px, src), device_id_type=MESH)

    def copy_b(s, part):
        to = lax.rem(px + s, PX)
        ks = pl.ds(part * KG, KG)
        return pltpu.make_async_remote_copy(
            src_ref=send_b.at[to, ks], dst_ref=recv_b.at[px, ks], send_sem=sb_sem.at[part, to],
            recv_sem=rb_sem.at[part, px], device_id=(to, py), device_id_type=MESH)

    def arrive_b(src, part):
        ks = pl.ds(part * KG, KG)
        return pltpu.make_async_remote_copy(
            src_ref=send_b.at[src, ks], dst_ref=recv_b.at[src, ks], send_sem=sb_sem.at[part, src],
            recv_sem=rb_sem.at[part, src], device_id=(src, py), device_id_type=MESH)

    def copy_m(to_x, h):
        return pltpu.make_async_remote_copy(
            src_ref=send_m.at[to_x, h], dst_ref=recv_m.at[py], send_sem=sm_sem.at[to_x, h], recv_sem=rm_sem.at[py],
            device_id=(to_x, 2 * px + h), device_id_type=MESH)

    def copy_n(to_y, r):
        return pltpu.make_async_remote_copy(
            src_ref=send_n.at[to_y, r], dst_ref=recv_n.at[px, py // 2], send_sem=sn_sem.at[to_y, r],
            recv_sem=rn_sem.at[px, py // 2], device_id=(4 * lax.rem(py, 2) + r, to_y), device_id_type=MESH)

    def own_n(to_y, r):
        return jnp.logical_and(4 * lax.rem(py, 2) + r == px, to_y == py)

    def arrive_n(src_x, t):
        return pltpu.make_async_remote_copy(
            src_ref=send_n.at[0, 0], dst_ref=recv_n.at[src_x, t], send_sem=sn_sem.at[0, 0],
            recv_sem=rn_sem.at[src_x, t], device_id=(src_x, 2 * t + px // 4), device_id_type=MESH)

    def copy_c(s):
        to = lax.rem(px + s, PX)
        return pltpu.make_async_remote_copy(
            src_ref=send_b.at[PX + to], dst_ref=recv_b.at[PX + px], send_sem=sc_sem.at[to], recv_sem=rc_sem.at[px],
            device_id=(to, py), device_id_type=MESH)

    def arrive_c(src):
        return pltpu.make_async_remote_copy(
            src_ref=send_b.at[PX + src], dst_ref=recv_b.at[PX + src], send_sem=sc_sem.at[src], recv_sem=rc_sem.at[src],
            device_id=(src, py), device_id_type=MESH)

    def copy_d(s, part):
        to = lax.rem(py + s, PY)
        ks = pl.ds(part * KG, KG)
        return pltpu.make_async_remote_copy(
            src_ref=send_a.at[PY + to, ks], dst_ref=lines_out.at[py, ks], send_sem=sd_sem.at[part, to],
            recv_sem=rd_sem.at[part, py], device_id=(px, to), device_id_type=MESH)

    def arrive_d(src, part):
        ks = pl.ds(part * KG, KG)
        return pltpu.make_async_remote_copy(
            src_ref=send_a.at[PY + src, ks], dst_ref=lines_out.at[src, ks], send_sem=sd_sem.at[part, src],
            recv_sem=rd_sem.at[part, src], device_id=(px, src), device_id_type=MESH)

    def z_forward(chunk):
        pltpu.make_async_copy(og.at[:, chunk], ogv.at[pl.ds(chunk * 4, 4)], og_sem.at[chunk]).wait()
        for jj in range(4):
            parts = []
            for j in (2 * jj, 2 * jj + 1):
                for b in range(4):
                    parts.append(ogv[chunk * 4 + b, pl.ds(j, 32, stride=8), :])
            rows = jnp.concatenate(parts, axis=0)
            high = rows.astype(BF)
            low = (rows - high.astype(F32)).astype(BF)
            both = dot_nt(zf[...], jnp.concatenate([high, low], axis=1))
            res = both[0:72] + both[72:144]
            blk[pl.ds(2 * jj, 72, stride=8), :] = res[:, 0:128]
            blk[pl.ds(2 * jj + 1, 72, stride=8), :] = res[:, 128:256]

    def step_a(s, c):
        to = lax.rem(py + s, PY)
        z_forward(to)
        send_a[to] = blk[0:528, :].reshape(KZ, 16, 128).astype(BF)

        @pl.when(s == 1)
        def _():
            pl.semaphore_wait(barrier, PX * PY - 1)

        copy_a(s).start()
        return c

    lax.fori_loop(1, PY, step_a, 0)
    z_forward(py)
    recv_a[py] = blk[0:528, :].reshape(KZ, 16, 128).astype(BF)

    def widen(k, c):
        rows = pl.ds(pl.multiple_of(k * 256, 256), 256)
        both = dot(xm[rows, :], dup[...])
        xr[rows, :] = both[:, 0:128]
        xi[rows, :] = both[:, 128:256]
        ogv[T1 + k] = jnp.zeros((256, 128), F32)
        ogv[T2 + k] = jnp.zeros((256, 128), F32)
        return c

    lax.fori_loop(0, 16, widen, 0)

    def wait_a(s, c):
        arrive_a(lax.rem(py + PY - s, PY)).wait_recv()
        return c

    lax.fori_loop(1, PY, wait_a, 0)

    def step_b(k, c):
        data = recv_a[0:PY, k].reshape(256, 128)
        both = dot(yf[...], data)
        res = (both[0:128] + both[128:256]).astype(BF)
        send_b[0:PX, k] = res.reshape(PX, 16, 128)
        return c

    def part_b(part, c):
        lax.fori_loop(part * KG, part * KG + KG, step_b, 0, unroll=True)

        def start_b(s, c2):
            copy_b(s, part).start()
            return c2

        return lax.fori_loop(1, PX, start_b, c)

    lax.fori_loop(0, 3, part_b, 0)
    pltpu.make_async_copy(xf_hbm, xfv, xf_sem).wait()

    def rows_c(data):
        data = data.astype(F32).reshape(KZ, 2, 8, 128)
        pad = jnp.zeros((8, 128), F32)
        parts = [jnp.concatenate([data[:, ri].reshape(264, 128), pad], axis=0).astype(BF) for ri in range(2)]
        lines[...] = jnp.concatenate(parts, axis=1)

    def term_c(src, cols):
        rows = pl.ds(pl.multiple_of(src * 256, 256), 256)
        return dot(lines[...], xfv[0, rows, cols]) + dot(lines[...], xfv[1, rows, cols])

    def arrive_c_rows(s):
        src = lax.rem(px + PX - s, PX)
        for part in range(3):
            arrive_b(src, part).wait_recv()
        rows_c(recv_b[src])
        return src

    rows_c(send_b[px])
    for k in range(4):
        sums[k] = term_c(px, slice(k * 256, k * 256 + 256))

    def step_gather(s, c):
        src = arrive_c_rows(s)
        for k in range(4):
            sums[k] = sums[k] + term_c(src, slice(k * 256, k * 256 + 256))
        return c

    lax.fori_loop(1, PX - 1, step_gather, 0)
    last_src = arrive_c_rows(PX - 1)

    def block_c(k):
        return lax.rem(px // 2 + py + k, 4)

    def step_c(k, c):
        pair = block_c(k)
        cols = pl.ds(pl.multiple_of(pair * 256, 256), 256)
        res = sums[pair] + term_c(last_src, cols)
        moved = dot(perm[...], res.astype(BF)).astype(BF)
        for e in range(2):
            send_m[2 * pair + e] = moved[:, e * 128:(e + 1) * 128].reshape(2, MR, 128)
        return c

    def chunks_c(k, act, act_own):
        for e in range(2):
            for h in range(2):
                to = 2 * block_c(k) + e
                own = jnp.logical_and(to == px, 2 * px + h == py)

                @pl.when(jnp.logical_not(own))
                def _():
                    act(to, h)

                @pl.when(own)
                def _():
                    act_own(to, h)

    def start_c(k, c):
        def own(to, h):
            local = pltpu.make_async_copy(send_m.at[to, h], recv_m.at[py], self_sem)
            local.start()
            local.wait()

        chunks_c(k, lambda to, h: copy_m(to, h).start(), own)
        return c

    def sent_c(k, c):
        chunks_c(k, lambda to, h: copy_m(to, h).wait_send(), lambda to, h: None)
        return c

    def first_c(k, c):
        step_c(k, c)
        return start_c(k, c)

    lax.fori_loop(0, 2, first_c, 0)
    lax.fori_loop(2, 4, step_c, 0)
    lax.fori_loop(0, 2, sent_c, 0)
    lax.fori_loop(2, 4, start_c, 0)

    def senders(k):
        first = lax.rem(px // 2 + 8 - owner_px // 2 - k, 4)
        return [first + 4 * m for m in range(4)]

    def place_modes(k):
        real, imag = [], []
        for src in senders(k):
            @pl.when(jnp.logical_not(jnp.logical_and(owner_px == px, src == py)))
            def _():
                pltpu.make_async_remote_copy(
                    src_ref=send_m.at[0, 0], dst_ref=recv_m.at[src], send_sem=sm_sem.at[0, 0], recv_sem=rm_sem.at[src],
                    device_id=(owner_px, src), device_id_type=MESH).wait_recv()

            turned = recv_m[src].astype(F32).T.astype(BF)
            real.append(turned[0:64])
            imag.append(turned[64:128])
        real, imag = jnp.concatenate(real, axis=0), jnp.concatenate(imag, axis=0)
        for r in range(4):
            cols = slice(r * 256, r * 256 + 256)
            res = dot(real, place[0, :, cols]) + dot(imag, place[1, :, cols])
            for m, src in enumerate(senders(k)):
                rows = pl.ds(r, 64, stride=4)
                ogv[G + src, rows, :] = res[m * 64:m * 64 + 64, 0:128]
                ogv[GS + src, rows, :] = res[m * 64:m * 64 + 64, 128:256]

    pltpu.make_async_copy(w_hbm, wv, w_sem).wait()

    def step_modes(pair, off, half):
        tv, uv = ogv.at[T1 + pair], ogv.at[T2 + pair]

        def add(k, acc):
            acc = list(acc)
            for src in senders(2 * half + k):
                gv, sv = ogv.at[G + src], ogv.at[GS + src]
                wp = [wv.at[2 * pair + ii, pl.ds(2 * src, 2)] for ii in range(2)]
                for oo in range(2):
                    w = [wp[ii][oo, off:off + 16, :].astype(F32) for ii in range(2)]
                    for b in range(4):
                        at = (b * 2 + oo) * 32 + off
                        gb = gv[at:at + 16, 0:66]
                        sb = sv[at:at + 16, 0:66]
                        for ii in range(2):
                            n = (ii * 4 + b) * 2
                            acc[n] = acc[n] + w[ii] * gb
                            acc[n + 1] = acc[n + 1] + w[ii] * sb
            return tuple(acc)

        places = [(ref, (b * 2 + ii) * 32 + off) for ii in range(2) for b in range(4) for ref in (tv, uv)]
        if half == 0:
            acc = tuple(jnp.zeros((16, 66), F32) for _ in places)
        else:
            acc = tuple(ref[at:at + 16, 0:66] for ref, at in places)
        acc = lax.fori_loop(0, 2, add, acc)
        for (ref, at), total in zip(places, acc):
            ref[at:at + 16, 0:66] = total

    def fold_modes(k):
        def rows_of(base, r):
            data = ogv[base + k, pl.ds(r, 64, stride=4), :]
            return data + pltpu.roll(data, 128 - KZ, 1)

        both = [jnp.concatenate([rows_of(T1, r), rows_of(T2, r)], axis=0).astype(BF) for r in range(4)]
        return dot_nt(back[...], jnp.concatenate(both, axis=0)).astype(BF)

    def send_modes(k):
        for e in range(4):
            r = lax.rem(px + e, 4)

            @pl.when(jnp.logical_not(own_n(k, r)))
            def _():
                copy_n(k, r).start()

            @pl.when(own_n(k, r))
            def _():
                local = pltpu.make_async_copy(send_n.at[k, r], recv_n.at[px, py // 2], self_sem)
                local.start()
                local.wait()

    def step_first(pair, c):
        step_modes(pair, 0, 0)
        step_modes(pair, 16, 0)
        return c

    def step_last(s, c):
        pairs = [lax.rem(py + 2 * s + e, PY) for e in range(2)]
        for pair in pairs:
            step_modes(pair, 0, 1)
            step_modes(pair, 16, 1)
        folded = [fold_modes(pair) for pair in pairs]
        for pair, chunk in zip(pairs, folded):
            for r in range(4):
                send_n[pair, r] = chunk[:, r * 128:(r + 1) * 128]
        for pair in pairs:
            send_modes(pair)
        return c

    place_modes(0)
    place_modes(1)
    lax.fori_loop(0, PY, step_first, 0)
    place_modes(2)
    place_modes(3)
    lax.fori_loop(0, PX, step_last, 0)

    def step_weight(i, c):
        for off in (0, 16):
            xrb = [xr[pl.ds(pl.multiple_of((b * 32 + i) * 32 + off, 16), 16), 0:66] for b in range(4)]
            xib = [xi[pl.ds(pl.multiple_of((b * 32 + i) * 32 + off, 16), 16), 0:66] for b in range(4)]

            def one(op, c2):
                gv, sv, out = ogv.at[G + op], ogv.at[GS + op], wv.at[i, pl.ds(2 * op, 2)]
                for oo in range(2):
                    total = None
                    for b in range(4):
                        at = (b * 2 + oo) * 32 + off
                        term = xrb[b] * gv[at:at + 16, 0:66] + xib[b] * sv[at:at + 16, 0:66]
                        total = term if total is None else total + term
                    out[oo, off:off + 16, :] = total.astype(BF)
                return c2

            lax.fori_loop(0, 16, one, 0)

        pltpu.make_async_copy(wv.at[i], wg.at[i], wg_sem.at[i]).start()
        return c

    lax.fori_loop(0, W1, step_weight, 0)

    def step_unplace(s, c):
        src = lax.rem(px + PX - s, PX)

        def wait_n(t, c2):
            @pl.when(jnp.logical_not(jnp.logical_and(src == px, 2 * t + px // 4 == py)))
            def _():
                arrive_n(src, t).wait_recv()

            return c2

        lax.fori_loop(0, 8, wait_n, 0)
        moved = dot(permt[...], recv_n[src].reshape(8 * NR, 128))
        dm[:, pl.ds(pl.multiple_of(src * 128, 128), 128)] = moved.astype(BF)
        return c

    lax.fori_loop(0, PX, step_unplace, 0)

    def x_inverse(to):
        rows = pl.ds(pl.multiple_of(to * 256, 256), 256)
        res = dot_nt(dm[...], xfv[0, rows, :]) + dot_nt(dm[...], xfv[1, rows, :])
        parts = [res[0:264, ri * 128:ri * 128 + 128].reshape(KZ, 8, 128) for ri in range(2)]
        return jnp.concatenate(parts, axis=1).astype(BF)

    def step_cb(s, c):
        to = lax.rem(px + s, PX)
        send_b[PX + to] = x_inverse(to)
        copy_c(s).start()
        return c

    lax.fori_loop(1, PX, step_cb, 0)
    recv_b[PX + px] = x_inverse(px)

    lax.fori_loop(W1, W2, step_weight, 0)

    def wait_c(s, c):
        arrive_c(lax.rem(px + PX - s, PX)).wait_recv()
        return c

    lax.fori_loop(1, PX, wait_c, 0)

    def step_bb(k, c):
        data = recv_b[PX:2 * PX, k].reshape(128, 128)
        res = dot(yi[...], jnp.concatenate([data, data], axis=0)).astype(BF)
        send_a[PY:2 * PY, k] = res.reshape(PY, 16, 128)
        return c

    def part_d(part, c):
        lax.fori_loop(part * KG, part * KG + KG, step_bb, 0, unroll=True)

        def start_d(s, c2):
            copy_d(s, part).start()
            return c2

        return lax.fori_loop(1, PY, start_d, c)

    lax.fori_loop(0, 3, part_d, 0)
    lax.fori_loop(W2, 32, step_weight, 0)

    own_lines = pltpu.make_async_copy(send_a.at[PY + py], lines_out.at[py], self_sem)
    own_lines.start()

    def step_d(s, c):
        for part in range(3):
            arrive_d(lax.rem(py + PY - s, PY), part).wait_recv()
        return c

    lax.fori_loop(1, PY, step_d, 0)
    own_lines.wait()

    def end_px(s, c):
        for part in range(3):
            copy_b(s, part).wait_send()
        copy_c(s).wait_send()
        return c

    def end_py(s, c):
        copy_a(s).wait_send()
        for part in range(3):
            copy_d(s, part).wait_send()
        return c

    def end_m(t, c):
        def end_n(r, c2):
            @pl.when(jnp.logical_not(own_n(t, r)))
            def _():
                copy_n(t, r).wait_send()

            return c2

        lax.fori_loop(0, 4, end_n, 0)
        return c

    def end_w(i, c):
        pltpu.make_async_copy(wv.at[i], wg.at[i], wg_sem.at[i]).wait()
        return c

    lax.fori_loop(1, PX, end_px, 0)
    lax.fori_loop(1, PY, end_py, 0)
    lax.fori_loop(2, 4, sent_c, 0)
    lax.fori_loop(0, PY, end_m, 0)
    lax.fori_loop(0, 32, end_w, 0)


def finish(held, lines, zi, wg, ig, buf, blk0, blk1, turn0, turn1, outv, in_sem, out_sem, ig_sem):
    def load(i):
        return pltpu.make_async_copy(held.at[pl.ds(2 * i, 2)], buf.at[pl.ds(2 * i, 2)], in_sem.at[i])

    def store(i):
        return pltpu.make_async_copy(buf.at[pl.ds(2 * i, 2)], wg.at[pl.ds(2 * i, 2)], out_sem.at[i])

    def start(i, c):
        load(i).start()
        return c

    lax.fori_loop(0, PY, start, 0)
    blk0[528:576, :] = jnp.zeros((48, 128), F32)
    blk1[528:576, :] = jnp.zeros((48, 128), F32)

    def step(k, c):
        slots = ((2 * k, blk0, turn0), (2 * k + 1, blk1, turn1))
        for src, blk, turn in slots:
            blk[0:528, :] = lines[src].astype(F32).reshape(528, 128)
        for j in range(8):
            for src, blk, turn in slots:
                turned = blk[pl.ds(j, 72, stride=8), :].T.astype(BF)
                turn[pl.ds(j, 128, stride=8), :] = dot(turned, zi[0]) + dot(turned, zi[1])
        for src, blk, turn in slots:
            outv[src] = turn[...].reshape(4, 256, 128).astype(BF)
        for src, blk, turn in slots:
            pltpu.make_async_copy(outv.at[src], ig.at[:, src], ig_sem.at[src]).start()

        @pl.when(k >= 3)
        def _():
            for e in range(2):
                load(2 * k - 6 + e).wait()
                store(2 * k - 6 + e).start()

        return c

    lax.fori_loop(0, PY // 2, step, 0)
    for i in range(10, 16):
        load(i).wait()
        store(i).start()

    def end(i, c):
        pltpu.make_async_copy(outv.at[i], ig.at[:, i], ig_sem.at[i]).wait()
        store(i).wait()
        return c

    lax.fori_loop(0, PY, end, 0)


def body(out_grad, input_modes, mode_weights):
    zf, zi, yf, yi, xf, perm, permt, place, back, dup = (jnp.asarray(t) for t in tables())
    og = out_grad.reshape(4, PY, 256, 128)
    xm = input_modes.reshape(4096, 66)
    w = mode_weights.reshape(32, 32, 32, 66)
    any_spec = pl.BlockSpec(memory_space=pl.ANY)
    vmem = pl.BlockSpec(memory_space=pltpu.VMEM)
    dma = pltpu.SemaphoreType.DMA
    held, lines = pl.pallas_call(
        kernel,
        out_shape=(
            jax.ShapeDtypeStruct((32, 32, 32, 66), BF),
            jax.ShapeDtypeStruct((PY, KZ, 16, 128), BF),
        ),
        in_specs=[any_spec, vmem, any_spec, any_spec] + [vmem] * 8,
        out_specs=(any_spec, any_spec),
        scratch_shapes=[
            pltpu.VMEM((4 * PY, 256, 128), F32),
            pltpu.VMEM((32, 32, 32, 66), BF),
            pltpu.VMEM((2, 2048, 1024), BF),
            pltpu.VMEM((2 * PY, KZ, 16, 128), BF),
            pltpu.VMEM((PY, KZ, 16, 128), BF),
            pltpu.VMEM((2 * PX, KZ, 16, 128), BF),
            pltpu.VMEM((2 * PX, KZ, 16, 128), BF),
            pltpu.VMEM((PX, 2, MR, 128), BF),
            pltpu.VMEM((PY, MR, 128), BF),
            pltpu.VMEM((PY, 4, NR, 128), BF),
            pltpu.VMEM((PX, 8, NR, 128), BF),
            pltpu.VMEM((CR, 256), BF),
            pltpu.VMEM((4, CR, 256), F32),
            pltpu.VMEM((CR, 1024), BF),
            pltpu.VMEM((4096, 128), F32),
            pltpu.VMEM((4096, 128), F32),
            pltpu.VMEM((576, 128), F32),
            dma((PY,)), dma, dma, dma((32,)), dma,
            dma((PY,)), dma((PY,)), dma((3, PX)), dma((3, PX)), dma((PX, 2)), dma((PY,)),
            dma((PY, 4)), dma((PX, 8)), dma((PX,)), dma((PX,)), dma((3, PY)), dma((3, PY)),
        ],
        compiler_params=pltpu.CompilerParams(
            collective_id=0, has_side_effects=True, vmem_limit_bytes=54 * 1024 * 1024
        ),
    )(og, xm, w, xf, zf, yf, yi, perm, permt, place, back, dup)
    wg, ig = pl.pallas_call(
        finish,
        out_shape=(
            jax.ShapeDtypeStruct((32, 32, 32, 66), BF),
            jax.ShapeDtypeStruct((4, PY, 256, 128), BF),
        ),
        in_specs=[any_spec, vmem, vmem],
        out_specs=(any_spec, any_spec),
        scratch_shapes=[
            pltpu.VMEM((32, 32, 32, 66), BF),
            pltpu.VMEM((576, 128), F32),
            pltpu.VMEM((576, 128), F32),
            pltpu.VMEM((1024, 128), F32),
            pltpu.VMEM((1024, 128), F32),
            pltpu.VMEM((PY, 4, 256, 128), BF),
            dma((PY,)), dma((PY,)), dma((PY,)),
        ],
        compiler_params=pltpu.CompilerParams(vmem_limit_bytes=54 * 1024 * 1024),
        cost_estimate=pl.CostEstimate(flops=600000000, bytes_accessed=23000000, transcendentals=0),
    )(held, lines, zi)
    return wg.reshape(32, 32, 8, 4, 66), ig.reshape(4, 32, 16, 8, 128)


def solution(mesh):
    spec = P(None, None, "px", "py", None)
    return jax.shard_map(
        body, mesh=mesh, in_specs=(spec, spec, spec), out_specs=(spec, spec), check_vma=False
    )
```

```python
import math

import jax
import jax.numpy as jnp
import ml_dtypes
import numpy as np
from jax import lax
from jax.experimental import pallas as pl
from jax.experimental.pallas import tpu as pltpu
from jax.sharding import PartitionSpec as P

BF = jnp.bfloat16
F32 = jnp.float32
MESH = pl.DeviceIdType.MESH
N = 128
KEPT = 64
KZ = 33
PX = 8
PY = 16
MR = 144
AHEAD = 4
W1, W2 = 5, 18
KG = 11
NR = 48
CR = 272
T1, T2, G, GS = 0, 16, 32, 48


def split(table):
    high = table.astype(ml_dtypes.bfloat16)
    low = (table - high.astype(np.float64)).astype(ml_dtypes.bfloat16)
    return high, low


def tables():
    bf = ml_dtypes.bfloat16
    grid = np.arange(N)
    angle_z = 2 * math.pi * (np.outer(np.arange(KZ), grid) % N) / N
    norm = 1.0 / math.sqrt(N)
    cz, sz = np.cos(angle_z) * norm, np.sin(angle_z) * norm
    kept = np.concatenate([np.arange(KEPT // 2), np.arange(N - KEPT // 2, N)])
    angle = 2 * math.pi * (np.outer(kept, grid) % N) / N
    cos, sin = np.cos(angle) * norm, np.sin(angle) * norm

    fz = np.stack([cz, -sz], axis=1).reshape(2 * KZ, N)
    hi, lo = split(fz)
    zf = np.zeros((144, 256), bf)
    zf[:66, :128] = hi
    zf[:66, 128:] = hi
    zf[72:138, :128] = lo
    weight = np.where(np.arange(KZ) == 0, 1.0, 2.0)[:, None]
    iz = np.stack([weight * cz, -weight * sz], axis=1).reshape(2 * KZ, N)
    hi, lo = split(iz)
    zi = np.zeros((2, 72, N), bf)
    zi[0, :66] = hi
    zi[1, :66] = lo

    full = np.zeros((2, KEPT, 2, N))
    full[0, :, 0] = cos
    full[0, :, 1] = sin
    full[1, :, 0] = -sin
    full[1, :, 1] = cos

    wy = full.reshape(2, PX, 8, 2, PY, 8).transpose(1, 0, 2, 4, 3, 5).reshape(128, 256)
    hi, lo = split(wy)
    yf = np.concatenate([hi, lo], axis=0)
    held = 4 * (2 * np.arange(8)[None, :] + np.arange(PX)[:, None] // 4) + np.arange(PX)[:, None] % 4
    wy = full[:, held.reshape(-1)].reshape(2, PX, 8, 2, PY, 8).transpose(1, 0, 2, 4, 3, 5).reshape(128, 256)
    hi, lo = split(wy)
    yi = np.concatenate([hi.T, lo.T], axis=1)

    wx = full.reshape(2, PX, 8, 2, PX, 16).transpose(4, 3, 5, 1, 0, 2)
    hi, lo = split(wx)
    xf = np.zeros((2, PX, 2, 8, 16, PX, 2, 8, 8), bf)
    for bc in range(8):
        xf[0, :, :, bc, :, :, :, bc, :] = hi
        xf[1, :, :, bc, :, :, :, bc, :] = lo
    xf = xf.reshape(2, 2048, 1024)

    perm = np.zeros((2, MR, CR), bf)
    for h in range(2):
        for k in range(KZ):
            for r in range(4):
                perm[h, 4 * k + r, 8 * k + 4 * h + r] = 1
    perm = perm.reshape(2 * MR, CR)
    permt = np.zeros((CR, 8, NR), bf)
    for t in range(8):
        for k in range(KZ):
            permt[8 * k + t, t, k] = 1
    permt = permt.reshape(CR, 8 * NR)

    place = np.zeros((2, MR, 4, 2, 128), bf)
    back = np.zeros((NR, 128), bf)
    for k in range(KZ):
        for r in range(4):
            place[0, 4 * k + r, r, 0, k] = 1
            place[1, 4 * k + r, r, 0, KZ + k] = 1
            place[1, 4 * k + r, r, 1, k] = 1
            place[0, 4 * k + r, r, 1, KZ + k] = -1
    place = place.reshape(2, MR, 1024)
    back[np.arange(KZ), np.arange(KZ)] = 1

    dup = np.zeros((2 * KZ, 2, 128), bf)
    for k in range(KZ):
        for part in range(2):
            dup[part * KZ + k, part, k] = 1
            dup[part * KZ + k, part, KZ + k] = 1
    dup = dup.reshape(2 * KZ, 256)
    return zf, zi, yf, yi, xf, perm, permt, place, back, dup


def dot(a, b):
    return jnp.dot(a, b, preferred_element_type=F32)


def dot_nt(a, b):
    return lax.dot_general(a, b, (((1,), (1,)), ((), ())), preferred_element_type=F32)


def kernel(
    og, xm, w_hbm, xf_hbm, zf, yf, yi, perm, permt, place, back, dup,
    wg, lines_out,
    ogv, wv, xfv, send_a, recv_a, send_b, recv_b, send_m, recv_m, send_n, recv_n,
    lines, sums, dm, xr, xi, blk,
    og_sem, w_sem, xf_sem, wg_sem, self_sem,
    sa_sem, ra_sem, sb_sem, rb_sem, sm_sem, rm_sem,
    sn_sem, rn_sem, sc_sem, rc_sem, sd_sem, rd_sem,
):
    px = lax.axis_index("px")
    py = lax.axis_index("py")
    owner_px = py // 2

    def load_og(s):
        chunk = lax.rem(py + s, PY)
        pltpu.make_async_copy(og.at[:, chunk], ogv.at[pl.ds(chunk * 4, 4)], og_sem.at[chunk]).start()

    for s in range(1, AHEAD + 1):
        load_og(s)

    barrier = pltpu.get_barrier_semaphore()
    me = px * PY + py

    def greet(k, c):
        to = lax.rem(me + k, PX * PY)
        pl.semaphore_signal(barrier, inc=1, device_id=(to // PY, lax.rem(to, PY)), device_id_type=MESH)
        return c

    lax.fori_loop(1, PX * PY, greet, 0)

    def copy_a(s):
        to = lax.rem(py + s, PY)
        return pltpu.make_async_remote_copy(
            src_ref=send_a.at[to], dst_ref=recv_a.at[py], send_sem=sa_sem.at[to], recv_sem=ra_sem.at[py],
            device_id=(px, to), device_id_type=MESH)

    def arrive_a(src):
        return pltpu.make_async_remote_copy(
            src_ref=send_a.at[src], dst_ref=recv_a.at[src], send_sem=sa_sem.at[src], recv_sem=ra_sem.at[src],
            device_id=(px, src), device_id_type=MESH)

    def copy_b(s, part):
        to = lax.rem(px + s, PX)
        ks = pl.ds(part * KG, KG)
        return pltpu.make_async_remote_copy(
            src_ref=send_b.at[to, ks], dst_ref=recv_b.at[px, ks], send_sem=sb_sem.at[part, to],
            recv_sem=rb_sem.at[part, px], device_id=(to, py), device_id_type=MESH)

    def arrive_b(src, part):
        ks = pl.ds(part * KG, KG)
        return pltpu.make_async_remote_copy(
            src_ref=send_b.at[src, ks], dst_ref=recv_b.at[src, ks], send_sem=sb_sem.at[part, src],
            recv_sem=rb_sem.at[part, src], device_id=(src, py), device_id_type=MESH)

    def copy_m(to_x, h):
        return pltpu.make_async_remote_copy(
            src_ref=send_m.at[to_x, h], dst_ref=recv_m.at[py], send_sem=sm_sem.at[to_x, h], recv_sem=rm_sem.at[py],
            device_id=(to_x, 2 * px + h), device_id_type=MESH)

    def copy_n(to_y, r):
        return pltpu.make_async_remote_copy(
            src_ref=send_n.at[to_y, r], dst_ref=recv_n.at[px, py // 2], send_sem=sn_sem.at[to_y, r],
            recv_sem=rn_sem.at[px, py // 2], device_id=(4 * lax.rem(py, 2) + r, to_y), device_id_type=MESH)

    def own_n(to_y, r):
        return jnp.logical_and(4 * lax.rem(py, 2) + r == px, to_y == py)

    def arrive_n(src_x, t):
        return pltpu.make_async_remote_copy(
            src_ref=send_n.at[0, 0], dst_ref=recv_n.at[src_x, t], send_sem=sn_sem.at[0, 0],
            recv_sem=rn_sem.at[src_x, t], device_id=(src_x, 2 * t + px // 4), device_id_type=MESH)

    def copy_c(s):
        to = lax.rem(px + s, PX)
        return pltpu.make_async_remote_copy(
            src_ref=send_b.at[PX + to], dst_ref=recv_b.at[PX + px], send_sem=sc_sem.at[to], recv_sem=rc_sem.at[px],
            device_id=(to, py), device_id_type=MESH)

    def arrive_c(src):
        return pltpu.make_async_remote_copy(
            src_ref=send_b.at[PX + src], dst_ref=recv_b.at[PX + src], send_sem=sc_sem.at[src], recv_sem=rc_sem.at[src],
            device_id=(src, py), device_id_type=MESH)

    def copy_d(s, part):
        to = lax.rem(py + s, PY)
        ks = pl.ds(part * KG, KG)
        return pltpu.make_async_remote_copy(
            src_ref=send_a.at[PY + to, ks], dst_ref=lines_out.at[py, ks], send_sem=sd_sem.at[part, to],
            recv_sem=rd_sem.at[part, py], device_id=(px, to), device_id_type=MESH)

    def arrive_d(src, part):
        ks = pl.ds(part * KG, KG)
        return pltpu.make_async_remote_copy(
            src_ref=send_a.at[PY + src, ks], dst_ref=lines_out.at[src, ks], send_sem=sd_sem.at[part, src],
            recv_sem=rd_sem.at[part, src], device_id=(px, src), device_id_type=MESH)

    def z_forward(chunk):
        pltpu.make_async_copy(og.at[:, chunk], ogv.at[pl.ds(chunk * 4, 4)], og_sem.at[chunk]).wait()
        for jj in range(4):
            parts = []
            for j in (2 * jj, 2 * jj + 1):
                for b in range(4):
                    parts.append(ogv[chunk * 4 + b, pl.ds(j, 32, stride=8), :])
            rows = jnp.concatenate(parts, axis=0)
            high = rows.astype(BF)
            low = (rows - high.astype(F32)).astype(BF)
            both = dot_nt(zf[...], jnp.concatenate([high, low], axis=1))
            res = both[0:72] + both[72:144]
            blk[pl.ds(2 * jj, 72, stride=8), :] = res[:, 0:128]
            blk[pl.ds(2 * jj + 1, 72, stride=8), :] = res[:, 128:256]

    def step_a(s, c):
        to = lax.rem(py + s, PY)

        @pl.when(s <= PY - AHEAD)
        def _():
            load_og(s + AHEAD)

        z_forward(to)
        send_a[to] = blk[0:528, :].reshape(KZ, 16, 128).astype(BF)

        @pl.when(s == 1)
        def _():
            pl.semaphore_wait(barrier, PX * PY - 1)

        copy_a(s).start()
        return c

    lax.fori_loop(1, PY, step_a, 0)
    pltpu.make_async_copy(xf_hbm, xfv, xf_sem).start()
    pltpu.make_async_copy(w_hbm, wv, w_sem).start()
    z_forward(py)
    recv_a[py] = blk[0:528, :].reshape(KZ, 16, 128).astype(BF)

    def widen(k, c):
        rows = pl.ds(pl.multiple_of(k * 256, 256), 256)
        both = dot(xm[rows, :], dup[...])
        xr[rows, :] = both[:, 0:128]
        xi[rows, :] = both[:, 128:256]
        ogv[T1 + k] = jnp.zeros((256, 128), F32)
        ogv[T2 + k] = jnp.zeros((256, 128), F32)
        return c

    lax.fori_loop(0, 16, widen, 0)

    def wait_a(s, c):
        arrive_a(lax.rem(py + PY - s, PY)).wait_recv()
        return c

    lax.fori_loop(1, PY, wait_a, 0)

    def step_b(k, c):
        data = recv_a[0:PY, k].reshape(256, 128)
        both = dot(yf[...], data)
        res = (both[0:128] + both[128:256]).astype(BF)
        send_b[0:PX, k] = res.reshape(PX, 16, 128)
        return c

    def part_b(part, c):
        lax.fori_loop(part * KG, part * KG + KG, step_b, 0, unroll=True)

        def start_b(s, c2):
            copy_b(s, part).start()
            return c2

        return lax.fori_loop(1, PX, start_b, c)

    lax.fori_loop(0, 3, part_b, 0)
    pltpu.make_async_copy(xf_hbm, xfv, xf_sem).wait()

    def rows_c(data):
        data = data.astype(F32).reshape(KZ, 2, 8, 128)
        pad = jnp.zeros((8, 128), F32)
        parts = [jnp.concatenate([data[:, ri].reshape(264, 128), pad], axis=0).astype(BF) for ri in range(2)]
        lines[...] = jnp.concatenate(parts, axis=1)

    def term_c(src, cols):
        rows = pl.ds(pl.multiple_of(src * 256, 256), 256)
        return dot(lines[...], xfv[0, rows, cols]) + dot(lines[...], xfv[1, rows, cols])

    def arrive_c_rows(s):
        src = lax.rem(px + PX - s, PX)
        for part in range(3):
            arrive_b(src, part).wait_recv()
        rows_c(recv_b[src])
        return src

    rows_c(send_b[px])
    for k in range(4):
        sums[k] = term_c(px, slice(k * 256, k * 256 + 256))

    def step_gather(s, c):
        src = arrive_c_rows(s)
        for k in range(4):
            sums[k] = sums[k] + term_c(src, slice(k * 256, k * 256 + 256))
        return c

    lax.fori_loop(1, PX - 1, step_gather, 0)
    last_src = arrive_c_rows(PX - 1)

    def block_c(k):
        return lax.rem(px // 2 + py + k, 4)

    def step_c(k, c):
        pair = block_c(k)
        cols = pl.ds(pl.multiple_of(pair * 256, 256), 256)
        res = sums[pair] + term_c(last_src, cols)
        moved = dot(perm[...], res.astype(BF)).astype(BF)
        for e in range(2):
            send_m[2 * pair + e] = moved[:, e * 128:(e + 1) * 128].reshape(2, MR, 128)
        return c

    def chunks_c(k, act, act_own):
        for e in range(2):
            for h in range(2):
                to = 2 * block_c(k) + e
                own = jnp.logical_and(to == px, 2 * px + h == py)

                @pl.when(jnp.logical_not(own))
                def _():
                    act(to, h)

                @pl.when(own)
                def _():
                    act_own(to, h)

    def start_c(k, c):
        def own(to, h):
            local = pltpu.make_async_copy(send_m.at[to, h], recv_m.at[py], self_sem)
            local.start()
            local.wait()

        chunks_c(k, lambda to, h: copy_m(to, h).start(), own)
        return c

    def sent_c(k, c):
        chunks_c(k, lambda to, h: copy_m(to, h).wait_send(), lambda to, h: None)
        return c

    def first_c(k, c):
        step_c(k, c)
        return start_c(k, c)

    lax.fori_loop(0, 2, first_c, 0)
    lax.fori_loop(2, 4, step_c, 0)
    lax.fori_loop(0, 2, sent_c, 0)
    lax.fori_loop(2, 4, start_c, 0)

    def senders(k):
        first = lax.rem(px // 2 + 8 - owner_px // 2 - k, 4)
        return [first + 4 * m for m in range(4)]

    def place_modes(k):
        real, imag = [], []
        for src in senders(k):
            @pl.when(jnp.logical_not(jnp.logical_and(owner_px == px, src == py)))
            def _():
                pltpu.make_async_remote_copy(
                    src_ref=send_m.at[0, 0], dst_ref=recv_m.at[src], send_sem=sm_sem.at[0, 0], recv_sem=rm_sem.at[src],
                    device_id=(owner_px, src), device_id_type=MESH).wait_recv()

            turned = recv_m[src].astype(F32).T.astype(BF)
            real.append(turned[0:64])
            imag.append(turned[64:128])
        real, imag = jnp.concatenate(real, axis=0), jnp.concatenate(imag, axis=0)
        for r in range(4):
            cols = slice(r * 256, r * 256 + 256)
            res = dot(real, place[0, :, cols]) + dot(imag, place[1, :, cols])
            for m, src in enumerate(senders(k)):
                rows = pl.ds(r, 64, stride=4)
                ogv[G + src, rows, :] = res[m * 64:m * 64 + 64, 0:128]
                ogv[GS + src, rows, :] = res[m * 64:m * 64 + 64, 128:256]

    pltpu.make_async_copy(w_hbm, wv, w_sem).wait()

    def step_modes(pair, off, half):
        tv, uv = ogv.at[T1 + pair], ogv.at[T2 + pair]

        def add(k, acc):
            acc = list(acc)
            for src in senders(2 * half + k):
                gv, sv = ogv.at[G + src], ogv.at[GS + src]
                wp = [wv.at[2 * pair + ii, pl.ds(2 * src, 2)] for ii in range(2)]
                for oo in range(2):
                    w = [wp[ii][oo, off:off + 16, :].astype(F32) for ii in range(2)]
                    for b in range(4):
                        at = (b * 2 + oo) * 32 + off
                        gb = gv[at:at + 16, 0:66]
                        sb = sv[at:at + 16, 0:66]
                        for ii in range(2):
                            n = (ii * 4 + b) * 2
                            acc[n] = acc[n] + w[ii] * gb
                            acc[n + 1] = acc[n + 1] + w[ii] * sb
            return tuple(acc)

        places = [(ref, (b * 2 + ii) * 32 + off) for ii in range(2) for b in range(4) for ref in (tv, uv)]
        if half == 0:
            acc = tuple(jnp.zeros((16, 66), F32) for _ in places)
        else:
            acc = tuple(ref[at:at + 16, 0:66] for ref, at in places)
        acc = lax.fori_loop(0, 2, add, acc)
        for (ref, at), total in zip(places, acc):
            ref[at:at + 16, 0:66] = total

    def fold_modes(k):
        def rows_of(base, r):
            data = ogv[base + k, pl.ds(r, 64, stride=4), :]
            return data + pltpu.roll(data, 128 - KZ, 1)

        both = [jnp.concatenate([rows_of(T1, r), rows_of(T2, r)], axis=0).astype(BF) for r in range(4)]
        return dot_nt(back[...], jnp.concatenate(both, axis=0)).astype(BF)

    def send_modes(k):
        for e in range(4):
            r = lax.rem(px + e, 4)

            @pl.when(jnp.logical_not(own_n(k, r)))
            def _():
                copy_n(k, r).start()

            @pl.when(own_n(k, r))
            def _():
                local = pltpu.make_async_copy(send_n.at[k, r], recv_n.at[px, py // 2], self_sem)
                local.start()
                local.wait()

    def step_first(pair, c):
        step_modes(pair, 0, 0)
        step_modes(pair, 16, 0)
        return c

    def step_last(s, c):
        pairs = [lax.rem(py + 2 * s + e, PY) for e in range(2)]
        for pair in pairs:
            step_modes(pair, 0, 1)
            step_modes(pair, 16, 1)
        folded = [fold_modes(pair) for pair in pairs]
        for pair, chunk in zip(pairs, folded):
            for r in range(4):
                send_n[pair, r] = chunk[:, r * 128:(r + 1) * 128]
        for pair in pairs:
            send_modes(pair)
        return c

    place_modes(0)
    place_modes(1)
    lax.fori_loop(0, PY, step_first, 0)
    place_modes(2)
    place_modes(3)
    lax.fori_loop(0, PX, step_last, 0)

    def step_weight(i, c):
        for off in (0, 16):
            xrb = [xr[pl.ds(pl.multiple_of((b * 32 + i) * 32 + off, 16), 16), 0:66] for b in range(4)]
            xib = [xi[pl.ds(pl.multiple_of((b * 32 + i) * 32 + off, 16), 16), 0:66] for b in range(4)]

            def one(op, c2):
                gv, sv, out = ogv.at[G + op], ogv.at[GS + op], wv.at[i, pl.ds(2 * op, 2)]
                for oo in range(2):
                    total = None
                    for b in range(4):
                        at = (b * 2 + oo) * 32 + off
                        term = xrb[b] * gv[at:at + 16, 0:66] + xib[b] * sv[at:at + 16, 0:66]
                        total = term if total is None else total + term
                    out[oo, off:off + 16, :] = total.astype(BF)
                return c2

            lax.fori_loop(0, 16, one, 0)

        pltpu.make_async_copy(wv.at[i], wg.at[i], wg_sem.at[i]).start()
        return c

    lax.fori_loop(0, W1, step_weight, 0)

    def step_unplace(s, c):
        src = lax.rem(px + PX - s, PX)

        def wait_n(t, c2):
            @pl.when(jnp.logical_not(jnp.logical_and(src == px, 2 * t + px // 4 == py)))
            def _():
                arrive_n(src, t).wait_recv()

            return c2

        lax.fori_loop(0, 8, wait_n, 0)
        return c

    lax.fori_loop(0, PX, step_unplace, 0)
    for k in range(4):
        data = jnp.concatenate([recv_n[2 * k + e].reshape(8 * NR, 128) for e in range(2)], axis=1)
        dm[:, k * 256:k * 256 + 256] = dot(permt[...], data).astype(BF)

    def x_inverse(to):
        rows = pl.ds(pl.multiple_of(to * 256, 256), 256)
        res = dot_nt(dm[...], xfv[0, rows, :]) + dot_nt(dm[...], xfv[1, rows, :])
        parts = [res[0:264, ri * 128:ri * 128 + 128].reshape(KZ, 8, 128) for ri in range(2)]
        return jnp.concatenate(parts, axis=1).astype(BF)

    def step_cb(s, c):
        to = lax.rem(px + s, PX)
        send_b[PX + to] = x_inverse(to)
        copy_c(s).start()
        return c

    lax.fori_loop(1, PX, step_cb, 0)
    recv_b[PX + px] = x_inverse(px)

    lax.fori_loop(W1, W2, step_weight, 0)

    def wait_c(s, c):
        arrive_c(lax.rem(px + PX - s, PX)).wait_recv()
        return c

    lax.fori_loop(1, PX, wait_c, 0)

    def step_bb(k, c):
        data = recv_b[PX:2 * PX, k].reshape(128, 128)
        res = dot(yi[...], jnp.concatenate([data, data], axis=0)).astype(BF)
        send_a[PY:2 * PY, k] = res.reshape(PY, 16, 128)
        return c

    def part_d(part, c):
        lax.fori_loop(part * KG, part * KG + KG, step_bb, 0, unroll=True)

        def start_d(s, c2):
            copy_d(s, part).start()
            return c2

        return lax.fori_loop(1, PY, start_d, c)

    lax.fori_loop(0, 3, part_d, 0)
    lax.fori_loop(W2, 32, step_weight, 0)

    own_lines = pltpu.make_async_copy(send_a.at[PY + py], lines_out.at[py], self_sem)
    own_lines.start()

    def step_d(s, c):
        for part in range(3):
            arrive_d(lax.rem(py + PY - s, PY), part).wait_recv()
        return c

    lax.fori_loop(1, PY, step_d, 0)
    own_lines.wait()

    def end_px(s, c):
        for part in range(3):
            copy_b(s, part).wait_send()
        copy_c(s).wait_send()
        return c

    def end_py(s, c):
        copy_a(s).wait_send()
        for part in range(3):
            copy_d(s, part).wait_send()
        return c

    def end_m(t, c):
        def end_n(r, c2):
            @pl.when(jnp.logical_not(own_n(t, r)))
            def _():
                copy_n(t, r).wait_send()

            return c2

        lax.fori_loop(0, 4, end_n, 0)
        return c

    def end_w(i, c):
        pltpu.make_async_copy(wv.at[i], wg.at[i], wg_sem.at[i]).wait()
        return c

    lax.fori_loop(1, PX, end_px, 0)
    lax.fori_loop(1, PY, end_py, 0)
    lax.fori_loop(2, 4, sent_c, 0)
    lax.fori_loop(0, PY, end_m, 0)
    lax.fori_loop(0, 32, end_w, 0)


def finish(held, lines, zi, wg, ig, buf, blk0, blk1, turn0, turn1, outv, in_sem, out_sem, ig_sem):
    def load(i):
        return pltpu.make_async_copy(held.at[pl.ds(2 * i, 2)], buf.at[pl.ds(2 * i, 2)], in_sem.at[i])

    def store(i):
        return pltpu.make_async_copy(buf.at[pl.ds(2 * i, 2)], wg.at[pl.ds(2 * i, 2)], out_sem.at[i])

    def start(i, c):
        load(i).start()
        return c

    lax.fori_loop(0, PY, start, 0)
    blk0[528:576, :] = jnp.zeros((48, 128), F32)
    blk1[528:576, :] = jnp.zeros((48, 128), F32)

    def step(k, c):
        slots = ((2 * k, blk0, turn0), (2 * k + 1, blk1, turn1))
        for src, blk, turn in slots:
            blk[0:528, :] = lines[src].astype(F32).reshape(528, 128)
        for j in range(8):
            for src, blk, turn in slots:
                turned = blk[pl.ds(j, 72, stride=8), :].T.astype(BF)
                turn[pl.ds(j, 128, stride=8), :] = dot(turned, zi[0]) + dot(turned, zi[1])
        for src, blk, turn in slots:
            outv[src] = turn[...].reshape(4, 256, 128).astype(BF)
        for src, blk, turn in slots:
            pltpu.make_async_copy(outv.at[src], ig.at[:, src], ig_sem.at[src]).start()

        @pl.when(k >= 3)
        def _():
            for e in range(2):
                load(2 * k - 6 + e).wait()
                store(2 * k - 6 + e).start()

        return c

    lax.fori_loop(0, PY // 2, step, 0)
    for i in range(10, 16):
        load(i).wait()
        store(i).start()

    def end(i, c):
        pltpu.make_async_copy(outv.at[i], ig.at[:, i], ig_sem.at[i]).wait()
        store(i).wait()
        return c

    lax.fori_loop(0, PY, end, 0)


def body(out_grad, input_modes, mode_weights):
    zf, zi, yf, yi, xf, perm, permt, place, back, dup = (jnp.asarray(t) for t in tables())
    og = out_grad.reshape(4, PY, 256, 128)
    xm = input_modes.reshape(4096, 66)
    w = mode_weights.reshape(32, 32, 32, 66)
    any_spec = pl.BlockSpec(memory_space=pl.ANY)
    vmem = pl.BlockSpec(memory_space=pltpu.VMEM)
    dma = pltpu.SemaphoreType.DMA
    held, lines = pl.pallas_call(
        kernel,
        out_shape=(
            jax.ShapeDtypeStruct((32, 32, 32, 66), BF),
            jax.ShapeDtypeStruct((PY, KZ, 16, 128), BF),
        ),
        in_specs=[any_spec, vmem, any_spec, any_spec] + [vmem] * 8,
        out_specs=(any_spec, any_spec),
        scratch_shapes=[
            pltpu.VMEM((4 * PY, 256, 128), F32),
            pltpu.VMEM((32, 32, 32, 66), BF),
            pltpu.VMEM((2, 2048, 1024), BF),
            pltpu.VMEM((2 * PY, KZ, 16, 128), BF),
            pltpu.VMEM((PY, KZ, 16, 128), BF),
            pltpu.VMEM((2 * PX, KZ, 16, 128), BF),
            pltpu.VMEM((2 * PX, KZ, 16, 128), BF),
            pltpu.VMEM((PX, 2, MR, 128), BF),
            pltpu.VMEM((PY, MR, 128), BF),
            pltpu.VMEM((PY, 4, NR, 128), BF),
            pltpu.VMEM((PX, 8, NR, 128), BF),
            pltpu.VMEM((CR, 256), BF),
            pltpu.VMEM((4, CR, 256), F32),
            pltpu.VMEM((CR, 1024), BF),
            pltpu.VMEM((4096, 128), F32),
            pltpu.VMEM((4096, 128), F32),
            pltpu.VMEM((576, 128), F32),
            dma((PY,)), dma, dma, dma((32,)), dma,
            dma((PY,)), dma((PY,)), dma((3, PX)), dma((3, PX)), dma((PX, 2)), dma((PY,)),
            dma((PY, 4)), dma((PX, 8)), dma((PX,)), dma((PX,)), dma((3, PY)), dma((3, PY)),
        ],
        compiler_params=pltpu.CompilerParams(
            collective_id=0, has_side_effects=True, vmem_limit_bytes=54 * 1024 * 1024
        ),
    )(og, xm, w, xf, zf, yf, yi, perm, permt, place, back, dup)
    wg, ig = pl.pallas_call(
        finish,
        out_shape=(
            jax.ShapeDtypeStruct((32, 32, 32, 66), BF),
            jax.ShapeDtypeStruct((4, PY, 256, 128), BF),
        ),
        in_specs=[any_spec, vmem, vmem],
        out_specs=(any_spec, any_spec),
        scratch_shapes=[
            pltpu.VMEM((32, 32, 32, 66), BF),
            pltpu.VMEM((576, 128), F32),
            pltpu.VMEM((576, 128), F32),
            pltpu.VMEM((1024, 128), F32),
            pltpu.VMEM((1024, 128), F32),
            pltpu.VMEM((PY, 4, 256, 128), BF),
            dma((PY,)), dma((PY,)), dma((PY,)),
        ],
        compiler_params=pltpu.CompilerParams(vmem_limit_bytes=54 * 1024 * 1024),
        cost_estimate=pl.CostEstimate(flops=600000000, bytes_accessed=23000000, transcendentals=0),
    )(held, lines, zi)
    return wg.reshape(32, 32, 8, 4, 66), ig.reshape(4, 32, 16, 8, 128)


def solution(mesh):
    spec = P(None, None, "px", "py", None)
    return jax.shard_map(
        body, mesh=mesh, in_specs=(spec, spec, spec), out_specs=(spec, spec), check_vma=False
    )
```

```python
import math

import jax
import jax.numpy as jnp
import ml_dtypes
import numpy as np
from jax import lax
from jax.experimental import pallas as pl
from jax.experimental.pallas import tpu as pltpu
from jax.sharding import PartitionSpec as P

BF = jnp.bfloat16
F32 = jnp.float32
MESH = pl.DeviceIdType.MESH
N = 128
KEPT = 64
KZ = 33
PX = 8
PY = 16
MR = 144
AHEAD = 4
W1, W2 = 5, 18
KG = 11
NR = 48
CR = 272
T1, T2, G, GS = 0, 16, 32, 48


def split(table):
    high = table.astype(ml_dtypes.bfloat16)
    low = (table - high.astype(np.float64)).astype(ml_dtypes.bfloat16)
    return high, low


def tables():
    bf = ml_dtypes.bfloat16
    grid = np.arange(N)
    angle_z = 2 * math.pi * (np.outer(np.arange(KZ), grid) % N) / N
    norm = 1.0 / math.sqrt(N)
    cz, sz = np.cos(angle_z) * norm, np.sin(angle_z) * norm
    kept = np.concatenate([np.arange(KEPT // 2), np.arange(N - KEPT // 2, N)])
    angle = 2 * math.pi * (np.outer(kept, grid) % N) / N
    cos, sin = np.cos(angle) * norm, np.sin(angle) * norm

    fz = np.stack([cz, -sz], axis=1).reshape(2 * KZ, N)
    hi, lo = split(fz)
    zf = np.zeros((144, 256), bf)
    zf[:66, :128] = hi
    zf[:66, 128:] = hi
    zf[72:138, :128] = lo
    weight = np.where(np.arange(KZ) == 0, 1.0, 2.0)[:, None]
    iz = np.stack([weight * cz, -weight * sz], axis=1).reshape(2 * KZ, N)
    hi, lo = split(iz)
    zi = np.zeros((2, 72, N), bf)
    zi[0, :66] = hi
    zi[1, :66] = lo

    full = np.zeros((2, KEPT, 2, N))
    full[0, :, 0] = cos
    full[0, :, 1] = sin
    full[1, :, 0] = -sin
    full[1, :, 1] = cos

    wy = full.reshape(2, PX, 8, 2, PY, 8).transpose(1, 0, 2, 4, 3, 5).reshape(128, 256)
    hi, lo = split(wy)
    yf = np.concatenate([hi, lo], axis=0)
    held = 4 * (2 * np.arange(8)[None, :] + np.arange(PX)[:, None] // 4) + np.arange(PX)[:, None] % 4
    wy = full[:, held.reshape(-1)].reshape(2, PX, 8, 2, PY, 8).transpose(1, 0, 2, 4, 3, 5).reshape(128, 256)
    hi, lo = split(wy)
    yi = np.concatenate([hi.T, lo.T], axis=1)

    wx = full.reshape(2, PX, 8, 2, PX, 16).transpose(4, 3, 5, 1, 0, 2)
    hi, lo = split(wx)
    xf = np.zeros((2, PX, 2, 8, 16, PX, 2, 8, 8), bf)
    for bc in range(8):
        xf[0, :, :, bc, :, :, :, bc, :] = hi
        xf[1, :, :, bc, :, :, :, bc, :] = lo
    xf = xf.reshape(2, 2048, 1024)

    perm = np.zeros((2, MR, CR), bf)
    for h in range(2):
        for k in range(KZ):
            for r in range(4):
                perm[h, 4 * k + r, 8 * k + 4 * h + r] = 1
    perm = perm.reshape(2 * MR, CR)
    permt = np.zeros((CR, 8, NR), bf)
    for t in range(8):
        for k in range(KZ):
            permt[8 * k + t, t, k] = 1
    permt = permt.reshape(CR, 8 * NR)

    place = np.zeros((2, MR, 4, 2, 128), bf)
    back = np.zeros((NR, 128), bf)
    for k in range(KZ):
        for r in range(4):
            place[0, 4 * k + r, r, 0, k] = 1
            place[1, 4 * k + r, r, 0, KZ + k] = 1
            place[1, 4 * k + r, r, 1, k] = 1
            place[0, 4 * k + r, r, 1, KZ + k] = -1
    place = place.reshape(2, MR, 1024)
    back[np.arange(KZ), np.arange(KZ)] = 1

    dup = np.zeros((2 * KZ, 2, 128), bf)
    for k in range(KZ):
        for part in range(2):
            dup[part * KZ + k, part, k] = 1
            dup[part * KZ + k, part, KZ + k] = 1
    dup = dup.reshape(2 * KZ, 256)
    return zf, zi, yf, yi, xf, perm, permt, place, back, dup


def dot(a, b):
    return jnp.dot(a, b, preferred_element_type=F32)


def dot_nt(a, b):
    return lax.dot_general(a, b, (((1,), (1,)), ((), ())), preferred_element_type=F32)


def kernel(
    og, xm, w_hbm, xf_hbm, zf, yf, yi, perm, permt, place, back, dup,
    wg, lines_out,
    ogv, wv, xfv, send_a, recv_a, send_b, recv_b, send_m, recv_m, send_n, recv_n,
    lines, sums, dm, xr, xi, blk,
    og_sem, w_sem, xf_sem, wg_sem, self_sem,
    sa_sem, ra_sem, sb_sem, rb_sem, sm_sem, rm_sem,
    sn_sem, rn_sem, sc_sem, rc_sem, sd_sem, rd_sem,
):
    px = lax.axis_index("px")
    py = lax.axis_index("py")
    owner_px = py // 2

    def load_og(s):
        chunk = lax.rem(py + s, PY)
        pltpu.make_async_copy(og.at[:, chunk], ogv.at[pl.ds(chunk * 4, 4)], og_sem.at[chunk]).start()

    for s in range(1, AHEAD + 1):
        load_og(s)

    barrier = pltpu.get_barrier_semaphore()
    me = px * PY + py

    def greet(k, c):
        to = lax.rem(me + k, PX * PY)
        pl.semaphore_signal(barrier, inc=1, device_id=(to // PY, lax.rem(to, PY)), device_id_type=MESH)
        return c

    lax.fori_loop(1, PX * PY, greet, 0)

    def copy_a(s):
        to = lax.rem(py + s, PY)
        return pltpu.make_async_remote_copy(
            src_ref=send_a.at[to], dst_ref=recv_a.at[py], send_sem=sa_sem.at[to], recv_sem=ra_sem.at[py],
            device_id=(px, to), device_id_type=MESH)

    def arrive_a(src):
        return pltpu.make_async_remote_copy(
            src_ref=send_a.at[src], dst_ref=recv_a.at[src], send_sem=sa_sem.at[src], recv_sem=ra_sem.at[src],
            device_id=(px, src), device_id_type=MESH)

    def copy_b(s, part):
        to = lax.rem(px + s, PX)
        ks = pl.ds(part * KG, KG)
        return pltpu.make_async_remote_copy(
            src_ref=send_b.at[to, ks], dst_ref=recv_b.at[px, ks], send_sem=sb_sem.at[part, to],
            recv_sem=rb_sem.at[part, px], device_id=(to, py), device_id_type=MESH)

    def arrive_b(src, part):
        ks = pl.ds(part * KG, KG)
        return pltpu.make_async_remote_copy(
            src_ref=send_b.at[src, ks], dst_ref=recv_b.at[src, ks], send_sem=sb_sem.at[part, src],
            recv_sem=rb_sem.at[part, src], device_id=(src, py), device_id_type=MESH)

    def copy_m(to_x, h):
        return pltpu.make_async_remote_copy(
            src_ref=send_m.at[to_x, h], dst_ref=recv_m.at[py], send_sem=sm_sem.at[to_x, h], recv_sem=rm_sem.at[py],
            device_id=(to_x, 2 * px + h), device_id_type=MESH)

    def copy_n(to_y, r):
        return pltpu.make_async_remote_copy(
            src_ref=send_n.at[to_y, r], dst_ref=recv_n.at[px, py // 2], send_sem=sn_sem.at[to_y, r],
            recv_sem=rn_sem.at[px, py // 2], device_id=(4 * lax.rem(py, 2) + r, to_y), device_id_type=MESH)

    def own_n(to_y, r):
        return jnp.logical_and(4 * lax.rem(py, 2) + r == px, to_y == py)

    def arrive_n(src_x, t):
        return pltpu.make_async_remote_copy(
            src_ref=send_n.at[0, 0], dst_ref=recv_n.at[src_x, t], send_sem=sn_sem.at[0, 0],
            recv_sem=rn_sem.at[src_x, t], device_id=(src_x, 2 * t + px // 4), device_id_type=MESH)

    def copy_c(s):
        to = lax.rem(px + s, PX)
        return pltpu.make_async_remote_copy(
            src_ref=send_b.at[PX + to], dst_ref=recv_b.at[PX + px], send_sem=sc_sem.at[to], recv_sem=rc_sem.at[px],
            device_id=(to, py), device_id_type=MESH)

    def arrive_c(src):
        return pltpu.make_async_remote_copy(
            src_ref=send_b.at[PX + src], dst_ref=recv_b.at[PX + src], send_sem=sc_sem.at[src], recv_sem=rc_sem.at[src],
            device_id=(src, py), device_id_type=MESH)

    def copy_d(s, part):
        to = lax.rem(py + s, PY)
        ks = pl.ds(part * KG, KG)
        return pltpu.make_async_remote_copy(
            src_ref=send_a.at[PY + to, ks], dst_ref=lines_out.at[py, ks], send_sem=sd_sem.at[part, to],
            recv_sem=rd_sem.at[part, py], device_id=(px, to), device_id_type=MESH)

    def arrive_d(src, part):
        ks = pl.ds(part * KG, KG)
        return pltpu.make_async_remote_copy(
            src_ref=send_a.at[PY + src, ks], dst_ref=lines_out.at[src, ks], send_sem=sd_sem.at[part, src],
            recv_sem=rd_sem.at[part, src], device_id=(px, src), device_id_type=MESH)

    def z_forward(chunk):
        pltpu.make_async_copy(og.at[:, chunk], ogv.at[pl.ds(chunk * 4, 4)], og_sem.at[chunk]).wait()
        for jj in range(4):
            parts = []
            for j in (2 * jj, 2 * jj + 1):
                for b in range(4):
                    parts.append(ogv[chunk * 4 + b, pl.ds(j, 32, stride=8), :])
            rows = jnp.concatenate(parts, axis=0)
            high = rows.astype(BF)
            low = (rows - high.astype(F32)).astype(BF)
            both = dot_nt(zf[...], jnp.concatenate([high, low], axis=1))
            res = both[0:72] + both[72:144]
            blk[pl.ds(2 * jj, 72, stride=8), :] = res[:, 0:128]
            blk[pl.ds(2 * jj + 1, 72, stride=8), :] = res[:, 128:256]

    def step_a(s, c):
        to = lax.rem(py + s, PY)

        @pl.when(s <= PY - AHEAD)
        def _():
            load_og(s + AHEAD)

        z_forward(to)
        send_a[to] = blk[0:528, :].reshape(KZ, 16, 128).astype(BF)

        @pl.when(s == 1)
        def _():
            pl.semaphore_wait(barrier, PX * PY - 1)

        copy_a(s).start()
        return c

    lax.fori_loop(1, PY, step_a, 0)
    pltpu.make_async_copy(xf_hbm, xfv, xf_sem).start()
    pltpu.make_async_copy(w_hbm, wv, w_sem).start()
    z_forward(py)
    recv_a[py] = blk[0:528, :].reshape(KZ, 16, 128).astype(BF)

    def widen(k, c):
        rows = pl.ds(pl.multiple_of(k * 256, 256), 256)
        both = dot(xm[rows, :], dup[...])
        xr[rows, :] = both[:, 0:128]
        xi[rows, :] = both[:, 128:256]
        ogv[T1 + k] = jnp.zeros((256, 128), F32)
        ogv[T2 + k] = jnp.zeros((256, 128), F32)
        return c

    lax.fori_loop(0, 16, widen, 0)

    def wait_a(s, c):
        arrive_a(lax.rem(py + PY - s, PY)).wait_recv()
        return c

    lax.fori_loop(1, PY, wait_a, 0)

    def step_b(k, c):
        data = recv_a[0:PY, k].reshape(256, 128)
        both = dot(yf[...], data)
        res = (both[0:128] + both[128:256]).astype(BF)
        send_b[0:PX, k] = res.reshape(PX, 16, 128)
        return c

    def part_b(part, c):
        lax.fori_loop(part * KG, part * KG + KG, step_b, 0, unroll=True)

        def start_b(s, c2):
            copy_b(s, part).start()
            return c2

        return lax.fori_loop(1, PX, start_b, c)

    lax.fori_loop(0, 3, part_b, 0)
    pltpu.make_async_copy(xf_hbm, xfv, xf_sem).wait()

    def rows_c(data):
        data = data.astype(F32).reshape(KZ, 2, 8, 128)
        pad = jnp.zeros((8, 128), F32)
        parts = [jnp.concatenate([data[:, ri].reshape(264, 128), pad], axis=0).astype(BF) for ri in range(2)]
        lines[...] = jnp.concatenate(parts, axis=1)

    def term_c(src, cols):
        rows = pl.ds(pl.multiple_of(src * 256, 256), 256)
        return dot(lines[...], xfv[0, rows, cols]) + dot(lines[...], xfv[1, rows, cols])

    def arrive_c_rows(s):
        src = lax.rem(px + PX - s, PX)
        for part in range(3):
            arrive_b(src, part).wait_recv()
        rows_c(recv_b[src])
        return src

    rows_c(send_b[px])
    for k in range(4):
        sums[k] = term_c(px, slice(k * 256, k * 256 + 256))

    def step_gather(s, c):
        src = arrive_c_rows(s)
        for k in range(4):
            sums[k] = sums[k] + term_c(src, slice(k * 256, k * 256 + 256))
        return c

    lax.fori_loop(1, PX - 1, step_gather, 0)
    last_src = arrive_c_rows(PX - 1)

    def block_c(k):
        return lax.rem(px // 2 + py + k, 4)

    def step_c(k, c):
        pair = block_c(k)
        cols = pl.ds(pl.multiple_of(pair * 256, 256), 256)
        res = sums[pair] + term_c(last_src, cols)
        moved = dot(perm[...], res.astype(BF)).astype(BF)
        for e in range(2):
            send_m[2 * pair + e] = moved[:, e * 128:(e + 1) * 128].reshape(2, MR, 128)
        return c

    def chunks_c(k, act, act_own):
        for e in range(2):
            for h in range(2):
                to = 2 * block_c(k) + e
                own = jnp.logical_and(to == px, 2 * px + h == py)

                @pl.when(jnp.logical_not(own))
                def _():
                    act(to, h)

                @pl.when(own)
                def _():
                    act_own(to, h)

    def start_c(k, c):
        def own(to, h):
            local = pltpu.make_async_copy(send_m.at[to, h], recv_m.at[py], self_sem)
            local.start()
            local.wait()

        chunks_c(k, lambda to, h: copy_m(to, h).start(), own)
        return c

    def sent_c(k, c):
        chunks_c(k, lambda to, h: copy_m(to, h).wait_send(), lambda to, h: None)
        return c

    def first_c(k, c):
        step_c(k, c)
        return start_c(k, c)

    lax.fori_loop(0, 2, first_c, 0)
    lax.fori_loop(2, 4, step_c, 0)
    lax.fori_loop(0, 2, sent_c, 0)
    lax.fori_loop(2, 4, start_c, 0)

    def senders(k):
        first = lax.rem(px // 2 + 8 - owner_px // 2 - k, 4)
        return [first + 4 * m for m in range(4)]

    def place_modes(k):
        real, imag = [], []
        for src in senders(k):
            @pl.when(jnp.logical_not(jnp.logical_and(owner_px == px, src == py)))
            def _():
                pltpu.make_async_remote_copy(
                    src_ref=send_m.at[0, 0], dst_ref=recv_m.at[src], send_sem=sm_sem.at[0, 0], recv_sem=rm_sem.at[src],
                    device_id=(owner_px, src), device_id_type=MESH).wait_recv()

            turned = recv_m[src].astype(F32).T.astype(BF)
            real.append(turned[0:64])
            imag.append(turned[64:128])
        real, imag = jnp.concatenate(real, axis=0), jnp.concatenate(imag, axis=0)
        for r in range(4):
            cols = slice(r * 256, r * 256 + 256)
            res = dot(real, place[0, :, cols]) + dot(imag, place[1, :, cols])
            for m, src in enumerate(senders(k)):
                rows = pl.ds(r, 64, stride=4)
                ogv[G + src, rows, :] = res[m * 64:m * 64 + 64, 0:128]
                ogv[GS + src, rows, :] = res[m * 64:m * 64 + 64, 128:256]

    pltpu.make_async_copy(w_hbm, wv, w_sem).wait()

    def step_modes(pair, off, half):
        tv, uv = ogv.at[T1 + pair], ogv.at[T2 + pair]

        def add(k, acc):
            acc = list(acc)
            for src in senders(2 * half + k):
                gv, sv = ogv.at[G + src], ogv.at[GS + src]
                wp = [wv.at[2 * pair + ii, pl.ds(2 * src, 2)] for ii in range(2)]
                for oo in range(2):
                    w = [wp[ii][oo, off:off + 16, :].astype(F32) for ii in range(2)]
                    for b in range(4):
                        at = (b * 2 + oo) * 32 + off
                        gb = gv[at:at + 16, 0:66]
                        sb = sv[at:at + 16, 0:66]
                        for ii in range(2):
                            n = (ii * 4 + b) * 2
                            acc[n] = acc[n] + w[ii] * gb
                            acc[n + 1] = acc[n + 1] + w[ii] * sb
            return tuple(acc)

        places = [(ref, (b * 2 + ii) * 32 + off) for ii in range(2) for b in range(4) for ref in (tv, uv)]
        if half == 0:
            acc = tuple(jnp.zeros((16, 66), F32) for _ in places)
        else:
            acc = tuple(ref[at:at + 16, 0:66] for ref, at in places)
        acc = lax.fori_loop(0, 2, add, acc)
        for (ref, at), total in zip(places, acc):
            ref[at:at + 16, 0:66] = total

    def fold_modes(k):
        def rows_of(base, r):
            data = ogv[base + k, pl.ds(r, 64, stride=4), :]
            return data + pltpu.roll(data, 128 - KZ, 1)

        both = [jnp.concatenate([rows_of(T1, r), rows_of(T2, r)], axis=0).astype(BF) for r in range(4)]
        return dot_nt(back[...], jnp.concatenate(both, axis=0)).astype(BF)

    def send_modes(k):
        for e in range(4):
            r = lax.rem(px + e, 4)

            @pl.when(jnp.logical_not(own_n(k, r)))
            def _():
                copy_n(k, r).start()

            @pl.when(own_n(k, r))
            def _():
                local = pltpu.make_async_copy(send_n.at[k, r], recv_n.at[px, py // 2], self_sem)
                local.start()
                local.wait()

    def step_first(pair, c):
        step_modes(pair, 0, 0)
        step_modes(pair, 16, 0)
        return c

    def step_last(s, c):
        pairs = [lax.rem(py + 2 * s + e, PY) for e in range(2)]
        for pair in pairs:
            step_modes(pair, 0, 1)
            step_modes(pair, 16, 1)
        folded = [fold_modes(pair) for pair in pairs]
        for pair, chunk in zip(pairs, folded):
            for r in range(4):
                send_n[pair, r] = chunk[:, r * 128:(r + 1) * 128]
        for pair in pairs:
            send_modes(pair)
        return c

    place_modes(0)
    place_modes(1)
    lax.fori_loop(0, PY, step_first, 0)
    place_modes(2)
    place_modes(3)
    lax.fori_loop(0, PX, step_last, 0)

    def step_weight(i, c):
        for off in (0, 16):
            xrb = [xr[pl.ds(pl.multiple_of((b * 32 + i) * 32 + off, 16), 16), 0:66] for b in range(4)]
            xib = [xi[pl.ds(pl.multiple_of((b * 32 + i) * 32 + off, 16), 16), 0:66] for b in range(4)]

            def one(op, c2):
                gv, sv, out = ogv.at[G + op], ogv.at[GS + op], wv.at[i, pl.ds(2 * op, 2)]
                for oo in range(2):
                    total = None
                    for b in range(4):
                        at = (b * 2 + oo) * 32 + off
                        term = xrb[b] * gv[at:at + 16, 0:66] + xib[b] * sv[at:at + 16, 0:66]
                        total = term if total is None else total + term
                    out[oo, off:off + 16, :] = total.astype(BF)
                return c2

            lax.fori_loop(0, 16, one, 0)

        pltpu.make_async_copy(wv.at[i], wg.at[i], wg_sem.at[i]).start()
        return c

    lax.fori_loop(0, W1, step_weight, 0)

    def step_unplace(s, c):
        src = lax.rem(px + PX - s, PX)

        def wait_n(t, c2):
            @pl.when(jnp.logical_not(jnp.logical_and(src == px, 2 * t + px // 4 == py)))
            def _():
                arrive_n(src, t).wait_recv()

            return c2

        lax.fori_loop(0, 8, wait_n, 0)
        return c

    lax.fori_loop(0, PX, step_unplace, 0)
    for k in range(4):
        data = jnp.concatenate([recv_n[2 * k + e].reshape(8 * NR, 128) for e in range(2)], axis=1)
        dm[:, k * 256:k * 256 + 256] = dot(permt[...], data).astype(BF)

    def x_inverse(to):
        rows = pl.ds(pl.multiple_of(to * 256, 256), 256)
        res = dot_nt(dm[...], xfv[0, rows, :]) + dot_nt(dm[...], xfv[1, rows, :])
        parts = [res[0:264, ri * 128:ri * 128 + 128].reshape(KZ, 8, 128) for ri in range(2)]
        return jnp.concatenate(parts, axis=1).astype(BF)

    def step_cb(s, c):
        to = lax.rem(px + s, PX)
        send_b[PX + to] = x_inverse(to)
        copy_c(s).start()
        return c

    lax.fori_loop(1, PX, step_cb, 0)
    recv_b[PX + px] = x_inverse(px)

    lax.fori_loop(W1, W2, step_weight, 0)

    def wait_c(s, c):
        arrive_c(lax.rem(px + PX - s, PX)).wait_recv()
        return c

    lax.fori_loop(1, PX, wait_c, 0)

    def step_bb(k, c):
        data = recv_b[PX:2 * PX, k].reshape(128, 128)
        res = dot(yi[...], jnp.concatenate([data, data], axis=0)).astype(BF)
        send_a[PY:2 * PY, k] = res.reshape(PY, 16, 128)
        return c

    def part_d(part, c):
        lax.fori_loop(part * KG, part * KG + KG, step_bb, 0, unroll=True)

        def start_d(s, c2):
            copy_d(s, part).start()
            return c2

        return lax.fori_loop(1, PY, start_d, c)

    lax.fori_loop(0, 3, part_d, 0)
    lax.fori_loop(W2, 32, step_weight, 0)

    own_lines = pltpu.make_async_copy(send_a.at[PY + py], lines_out.at[py], self_sem)
    own_lines.start()

    def step_d(s, c):
        for part in range(3):
            arrive_d(lax.rem(py + PY - s, PY), part).wait_recv()
        return c

    lax.fori_loop(1, PY, step_d, 0)
    own_lines.wait()

    def end_px(s, c):
        for part in range(3):
            copy_b(s, part).wait_send()
        copy_c(s).wait_send()
        return c

    def end_py(s, c):
        copy_a(s).wait_send()
        for part in range(3):
            copy_d(s, part).wait_send()
        return c

    def end_m(t, c):
        def end_n(r, c2):
            @pl.when(jnp.logical_not(own_n(t, r)))
            def _():
                copy_n(t, r).wait_send()

            return c2

        lax.fori_loop(0, 4, end_n, 0)
        return c

    def end_w(i, c):
        pltpu.make_async_copy(wv.at[i], wg.at[i], wg_sem.at[i]).wait()
        return c

    lax.fori_loop(1, PX, end_px, 0)
    lax.fori_loop(1, PY, end_py, 0)
    lax.fori_loop(2, 4, sent_c, 0)
    lax.fori_loop(0, PY, end_m, 0)
    lax.fori_loop(0, 32, end_w, 0)


def finish(held, lines, zi, wg, ig, buf, blk0, blk1, turn0, turn1, outv, in_sem, out_sem, ig_sem):
    def load(i):
        return pltpu.make_async_copy(held.at[pl.ds(2 * i, 2)], buf.at[pl.ds(2 * i, 2)], in_sem.at[i])

    def store(i):
        return pltpu.make_async_copy(buf.at[pl.ds(2 * i, 2)], wg.at[pl.ds(2 * i, 2)], out_sem.at[i])

    def start(i, c):
        load(i).start()
        return c

    lax.fori_loop(0, PY, start, 0)
    blk0[528:576, :] = jnp.zeros((48, 128), F32)
    blk1[528:576, :] = jnp.zeros((48, 128), F32)

    def step(k, c):
        slots = ((2 * k, blk0, turn0), (2 * k + 1, blk1, turn1))
        for src, blk, turn in slots:
            blk[0:528, :] = lines[src].astype(F32).reshape(528, 128)
        for j in range(8):
            for src, blk, turn in slots:
                turned = blk[pl.ds(j, 72, stride=8), :].T.astype(BF)
                turn[pl.ds(j, 128, stride=8), :] = dot(turned, zi[0]) + dot(turned, zi[1])
        for src, blk, turn in slots:
            outv[src] = turn[...].reshape(4, 256, 128).astype(BF)
        for src, blk, turn in slots:
            pltpu.make_async_copy(outv.at[src], ig.at[:, src], ig_sem.at[src]).start()

        @pl.when(jnp.logical_and(k >= 3, k < 7))
        def _():
            for e in range(4):
                load(4 * k - 12 + e).wait()
                store(4 * k - 12 + e).start()

        return c

    lax.fori_loop(0, PY // 2, step, 0)

    def end(i, c):
        pltpu.make_async_copy(outv.at[i], ig.at[:, i], ig_sem.at[i]).wait()
        store(i).wait()
        return c

    lax.fori_loop(0, PY, end, 0)


def body(out_grad, input_modes, mode_weights):
    zf, zi, yf, yi, xf, perm, permt, place, back, dup = (jnp.asarray(t) for t in tables())
    og = out_grad.reshape(4, PY, 256, 128)
    xm = input_modes.reshape(4096, 66)
    w = mode_weights.reshape(32, 32, 32, 66)
    any_spec = pl.BlockSpec(memory_space=pl.ANY)
    vmem = pl.BlockSpec(memory_space=pltpu.VMEM)
    dma = pltpu.SemaphoreType.DMA
    held, lines = pl.pallas_call(
        kernel,
        out_shape=(
            jax.ShapeDtypeStruct((32, 32, 32, 66), BF),
            jax.ShapeDtypeStruct((PY, KZ, 16, 128), BF),
        ),
        in_specs=[any_spec, vmem, any_spec, any_spec] + [vmem] * 8,
        out_specs=(any_spec, any_spec),
        scratch_shapes=[
            pltpu.VMEM((4 * PY, 256, 128), F32),
            pltpu.VMEM((32, 32, 32, 66), BF),
            pltpu.VMEM((2, 2048, 1024), BF),
            pltpu.VMEM((2 * PY, KZ, 16, 128), BF),
            pltpu.VMEM((PY, KZ, 16, 128), BF),
            pltpu.VMEM((2 * PX, KZ, 16, 128), BF),
            pltpu.VMEM((2 * PX, KZ, 16, 128), BF),
            pltpu.VMEM((PX, 2, MR, 128), BF),
            pltpu.VMEM((PY, MR, 128), BF),
            pltpu.VMEM((PY, 4, NR, 128), BF),
            pltpu.VMEM((PX, 8, NR, 128), BF),
            pltpu.VMEM((CR, 256), BF),
            pltpu.VMEM((4, CR, 256), F32),
            pltpu.VMEM((CR, 1024), BF),
            pltpu.VMEM((4096, 128), F32),
            pltpu.VMEM((4096, 128), F32),
            pltpu.VMEM((576, 128), F32),
            dma((PY,)), dma, dma, dma((32,)), dma,
            dma((PY,)), dma((PY,)), dma((3, PX)), dma((3, PX)), dma((PX, 2)), dma((PY,)),
            dma((PY, 4)), dma((PX, 8)), dma((PX,)), dma((PX,)), dma((3, PY)), dma((3, PY)),
        ],
        compiler_params=pltpu.CompilerParams(
            collective_id=0, has_side_effects=True, vmem_limit_bytes=54 * 1024 * 1024
        ),
    )(og, xm, w, xf, zf, yf, yi, perm, permt, place, back, dup)
    wg, ig = pl.pallas_call(
        finish,
        out_shape=(
            jax.ShapeDtypeStruct((32, 32, 32, 66), BF),
            jax.ShapeDtypeStruct((4, PY, 256, 128), BF),
        ),
        in_specs=[any_spec, vmem, vmem],
        out_specs=(any_spec, any_spec),
        scratch_shapes=[
            pltpu.VMEM((32, 32, 32, 66), BF),
            pltpu.VMEM((576, 128), F32),
            pltpu.VMEM((576, 128), F32),
            pltpu.VMEM((1024, 128), F32),
            pltpu.VMEM((1024, 128), F32),
            pltpu.VMEM((PY, 4, 256, 128), BF),
            dma((PY,)), dma((PY,)), dma((PY,)),
        ],
        compiler_params=pltpu.CompilerParams(vmem_limit_bytes=54 * 1024 * 1024),
        cost_estimate=pl.CostEstimate(flops=600000000, bytes_accessed=23000000, transcendentals=0),
    )(held, lines, zi)
    return wg.reshape(32, 32, 8, 4, 66), ig.reshape(4, 32, 16, 8, 128)


def solution(mesh):
    spec = P(None, None, "px", "py", None)
    return jax.shard_map(
        body, mesh=mesh, in_specs=(spec, spec, spec), out_specs=(spec, spec), check_vma=False
    )
```
